128 devices in a mesh: coarse: 4 (over y_lo, core), sector: 32 (over y_hi, x, z).
Axes of the slice: x: 4, y: 4 (y_hi: 2, y_lo: 2; y = y_hi * 2 + y_lo), z: 4, core: 2. Of those that a mesh axis runs over, the one named last changes fastest.
Arguments:
- fine_populations: float32 [19, 128, 512, 128], P(None, 'coarse', 'sector'), as said below
- coarse_face: float32 [2, 19, 16384], P(None, None, ('coarse', 'sector')), as said below
- ghost_map: int32 [128, 512], P('coarse', 'sector'), may hold values from 0 to 255, as said below
- marker_force: bfloat16 [4096, 3, 128], P(('coarse', 'sector')), may hold values from -6 to 6
- marker_weights: bfloat16 [4096, 128, 128], P(('coarse', 'sector')), may hold values from 0 to 0.015625
- marker_tiles: int32 [4096], P(('coarse', 'sector')), may hold values from 0 to 575, as said below
- block_counts: int32 [128], P(('coarse', 'sector')), may hold values from 4 to 32, as said below
Outputs:
- fine_state: float32 [19, 128, 512, 128], P(None, 'coarse', 'sector')
The draws below stay inside these ranges and needn't reach their ends.
Inputs may be any that keep to these rules, and one draw needn't show every extreme that they name: `fine_populations`: each population is its lattice weight w_i times a factor between 0.5 and 2. `coarse_face`: each population is its lattice weight w_i times a factor between 0.5 and 2. `ghost_map`: an index into the 128 coarse interface cells of the same device followed by the 128 of the next device along sector, the last device's next being the first. `marker_tiles`: a tile of the block's own device, possibly lying one cell past either azimuthal end of its cells. `block_counts`: some device has all 32 blocks live.
All inputs are finite; a program needn't handle non-finite values.
Results may differ from the reference program's by a relative error of at most 0.0003.
Values sent between devices are 32-bit elements; how exact they have to be, the bound alone decides.
A program may use at most 64 MiB of HBM per device.

```python
import math
import jax
import jax.numpy as jnp
from jax import lax

FA = 32
FR = 16
FW = 128
TA = 1
TR = 1
TW = 128
NB = 32
MB = 128
TILE = 128
GR = 8
GCELLS = 128
NA = 128
NR = 512
NTILE = 576
BLOCKS = 4096
CELLS_C = 16384
N_SECTOR = 32


LATTICE_WEIGHTS = (1.0 / 3.0,) + (1.0 / 18.0,) * 6 + (1.0 / 36.0,) * 12


def population_factor(key, shape):
    return jnp.exp(jax.random.uniform(key, shape, jnp.float32, -math.log(2.0), math.log(2.0)))


def draw_fine_populations(key, part):
    weights = jnp.array(LATTICE_WEIGHTS, jnp.float32).reshape(19, 1, 1, 1)
    return weights * population_factor(key, (19, NA, NR, FW))


def draw_coarse_face(key, part):
    weights = jnp.array(LATTICE_WEIGHTS, jnp.float32).reshape(1, 19, 1)
    return weights * population_factor(key, (2, 19, CELLS_C))


def draw_ghost_map(key, part):
    devices_axial = NA // FA
    devices_cycle = NR // FR
    offsets = jax.random.randint(jax.random.fold_in(key, 1), (devices_axial * devices_cycle,), 0, GR + 1)
    shuffled = jax.random.permutation(jax.random.fold_in(key, 2), devices_axial * devices_cycle)
    offsets = offsets.at[shuffled[0]].set(0).at[shuffled[1]].set(GR)
    offsets = offsets.reshape(devices_axial, devices_cycle)
    row_pos = jnp.arange(NA, dtype=jnp.int32)[:, None]
    col_pos = jnp.arange(NR, dtype=jnp.int32)[None, :]
    coarse_row = row_pos % FA // 2
    column = offsets[row_pos // FA, col_pos // FR] + col_pos % FR // 2
    mapped = jnp.where(column < GR, coarse_row * GR + column, GCELLS + coarse_row * GR + column - GR)
    return mapped.astype(jnp.int32)


def draw_marker_tiles(key, part):
    tiles = jax.random.randint(jax.random.fold_in(key, 3), (BLOCKS,), 0, NTILE)
    shuffled = jax.random.permutation(jax.random.fold_in(key, 4), BLOCKS)
    tiles = tiles.at[shuffled[0]].set(0).at[shuffled[1]].set(NTILE - 1)
    return tiles.astype(jnp.int32)


def draw_block_counts(key, part):
    devices = BLOCKS // NB
    counts = jax.random.randint(jax.random.fold_in(key, 5), (devices,), NB // 8, NB // 2 + 1)
    shuffled = jax.random.permutation(jax.random.fold_in(key, 6), devices)
    counts = counts.at[shuffled[0]].set(NB).at[shuffled[1]].set(NB // 8)
    return counts.astype(jnp.int32)


def levels(stream_key, shape, pieces, least, high):
    def one(dim, shards_of):
        heights = jax.random.uniform(jax.random.fold_in(jax.random.fold_in(stream_key, 6), dim), (shards_of,), jnp.float32, least / len(pieces), high / len(pieces))
        return jnp.repeat(jnp.exp(heights), shape[dim] // shards_of).reshape((-1,) + (1,) * (len(shape) - dim - 1))

    level = one(*pieces[0])
    for cut in pieces[1:]:
        level = level * one(*cut)
    return level


def centred(rng, shape, width, bound, cuts=(), kind=jnp.bfloat16):
    result = jax.random.normal(rng, shape, jnp.float32) * width
    if len(cuts) > 0:
        result = levels(rng, shape, cuts, -0.22, 0.18) * result
    return jnp.clip(result, min=-bound, max=bound).astype(kind)


def setup_inputs(seed: int = 0) -> dict:
    key_list = jax.random.split(jax.random.key(seed), 8)
    fine_populations = draw_fine_populations(jax.random.fold_in(key_list[7], 71), 0)
    coarse_face = draw_coarse_face(jax.random.fold_in(key_list[7], 71), 0)
    ghost_map = draw_ghost_map(jax.random.fold_in(key_list[7], 71), 0)
    marker_force = centred(key_list[3], (BLOCKS, 3, MB), 1.5, 6.0, ((0, 128),))
    marker_weights = jnp.clip(0.015625 * jax.random.uniform(key_list[4], (BLOCKS, MB, TILE), jnp.float32) ** levels(key_list[4], (BLOCKS, MB, TILE), ((0, 128),), -0.2, 0.2), 0.0, 0.015625).astype(jnp.bfloat16)
    marker_tiles = draw_marker_tiles(jax.random.fold_in(key_list[7], 71), 0)
    block_counts = draw_block_counts(jax.random.fold_in(key_list[7], 71), 0)
    return dict(fine_populations=fine_populations, coarse_face=coarse_face, ghost_map=ghost_map, marker_force=marker_force, marker_weights=marker_weights, marker_tiles=marker_tiles, block_counts=block_counts)


VELOCITIES = ((0, 0, 0), (1, 0, 0), (-1, 0, 0), (0, 1, 0), (0, -1, 0), (0, 0, 1), (0, 0, -1),
              (1, 1, 0), (-1, -1, 0), (1, -1, 0), (-1, 1, 0), (1, 0, 1), (-1, 0, -1), (1, 0, -1), (-1, 0, 1),
              (0, 1, 1), (0, -1, -1), (0, 1, -1), (0, -1, 1))
LATTICE_WEIGHTS = (1.0 / 3.0,) + (1.0 / 18.0,) * 6 + (1.0 / 36.0,) * 12
TAU_FINE = 0.8
TAU_COARSE = 0.65
FORCE_FACTOR = 1.0 - 0.5 / TAU_FINE
RESCALE = TAU_FINE / (2.0 * TAU_COARSE)


def opposite(pop_index):
    if pop_index == 0:
        return 0
    return pop_index + 1 if pop_index % 2 == 1 else pop_index - 1


def project(vector, pop_index):
    running = jnp.zeros_like(vector[0])
    for axis_index in range(3):
        component = VELOCITIES[pop_index][axis_index]
        if component == 1:
            running = running + vector[axis_index]
        elif component == -1:
            running = running - vector[axis_index]
    return running


def moments(populations):
    density = populations[0]
    for pop_index in range(1, 19):
        density = density + populations[pop_index]
    momentum = []
    for axis_index in range(3):
        running = jnp.zeros_like(density)
        for pop_index in range(19):
            component = VELOCITIES[pop_index][axis_index]
            if component == 1:
                running = running + populations[pop_index]
            elif component == -1:
                running = running - populations[pop_index]
        momentum.append(running)
    return density, momentum


def collide(populations, force_field):
    density, momentum = moments(populations)
    velocity = [(momentum[axis_index] + 0.5 * force_field[axis_index]) / density for axis_index in range(3)]
    speed_sq = velocity[0] * velocity[0] + velocity[1] * velocity[1] + velocity[2] * velocity[2]
    along_force = velocity[0] * force_field[0] + velocity[1] * force_field[1] + velocity[2] * force_field[2]
    results = []
    for pop_index in range(19):
        dotted = project(velocity, pop_index)
        pushed = project([force_field[0], force_field[1], force_field[2]], pop_index)
        weight = LATTICE_WEIGHTS[pop_index]
        balance = weight * density * (1.0 + 3.0 * dotted + 4.5 * dotted * dotted - 1.5 * speed_sq)
        source = FORCE_FACTOR * weight * (3.0 * (pushed - along_force) + 9.0 * dotted * pushed)
        results.append(populations[pop_index] - (populations[pop_index] - balance) / TAU_FINE + source)
    return jnp.stack(results)


def interface_values(coarse_pops):
    density, momentum = moments(coarse_pops)
    velocity = [momentum[axis_index] / density for axis_index in range(3)]
    speed_sq = velocity[0] * velocity[0] + velocity[1] * velocity[1] + velocity[2] * velocity[2]
    results = []
    for pop_index in range(19):
        dotted = project(velocity, pop_index)
        weight = LATTICE_WEIGHTS[pop_index]
        balance = weight * density * (1.0 + 3.0 * dotted + 4.5 * dotted * dotted - 1.5 * speed_sq)
        results.append(balance + RESCALE * (coarse_pops[pop_index] - balance))
    return jnp.stack(results)


def stream(relaxed, ghost_pops):
    cells_axial, cells_cycle, cells_radial = relaxed.shape[1:]
    axial_pos = jnp.arange(cells_axial)[:, None, None]
    radial_pos = jnp.arange(cells_radial)[None, None, :]
    results = []
    for pop_index in range(19):
        step_axial, step_cycle, step_radial = VELOCITIES[pop_index]
        shifted = relaxed[pop_index]
        if step_axial == 1:
            shifted = jnp.concatenate([jnp.zeros_like(shifted[:1]), shifted[:-1]], axis=0)
        elif step_axial == -1:
            shifted = jnp.concatenate([shifted[1:], jnp.zeros_like(shifted[:1])], axis=0)
        if step_cycle != 0:
            shifted = jnp.roll(shifted, step_cycle, axis=1)
        if step_radial == 1:
            shifted = jnp.concatenate([jnp.zeros_like(shifted[:, :, :1]), shifted[:, :, :-1]], axis=2)
        elif step_radial == -1:
            shifted = jnp.concatenate([shifted[:, :, 1:], jnp.zeros_like(shifted[:, :, :1])], axis=2)
        reflected = relaxed[opposite(pop_index)]
        if step_radial == 1:
            shifted = jnp.where(radial_pos == 0, reflected, shifted)
        elif step_radial == -1:
            shifted = jnp.where(radial_pos == cells_radial - 1, ghost_pops[pop_index][:, :, None], shifted)
        if step_axial == 1:
            shifted = jnp.where(axial_pos == 0, reflected, shifted)
        elif step_axial == -1:
            shifted = jnp.where(axial_pos == cells_axial - 1, reflected, shifted)
        results.append(shifted)
    return jnp.stack(results)


def reference(fine_populations, coarse_face, ghost_map, marker_force, marker_weights, marker_tiles, block_counts):
    contrib = jnp.einsum("bkm,bmx->bkx", marker_force.astype(jnp.float32), marker_weights.astype(jnp.float32),
                         precision=lax.Precision.HIGHEST)
    block_ids = jnp.arange(BLOCKS).astype(jnp.int32)
    device = block_ids // NB
    live_mask = (block_ids % NB) < block_counts[device]
    contrib = jnp.where(live_mask[:, None, None], contrib, 0.0)
    tiles_cycle = FR // TR + 2
    tiles_radial = FW // TW
    tile_id = marker_tiles.astype(jnp.int32)
    tile_axial = tile_id // (tiles_cycle * tiles_radial)
    tile_cycle = (tile_id // tiles_radial) % tiles_cycle
    tile_radial = tile_id % tiles_radial
    cell_pos = jnp.arange(TILE).astype(jnp.int32)
    cell_axial = cell_pos // (TR * TW)
    cell_cycle = (cell_pos // TW) % TR
    cell_radial = cell_pos % TW
    global_axial = ((device // N_SECTOR) * FA + tile_axial * TA)[:, None] + cell_axial[None, :]
    global_cycle = (((device % N_SECTOR) * FR + (tile_cycle - 1) * TR)[:, None] + cell_cycle[None, :]) % NR
    global_radial = (tile_radial * TW)[:, None] + cell_radial[None, :]
    flat_index = ((global_axial * NR + global_cycle) * FW + global_radial).astype(jnp.int32)
    force_field = jnp.zeros((3, NA * NR * FW), jnp.float32)
    force_field = force_field.at[:, flat_index.reshape(-1)].add(jnp.transpose(contrib, (1, 0, 2)).reshape(3, -1))
    force_field = force_field.reshape(3, NA, NR, FW)

    row_pos = jnp.arange(NA).astype(jnp.int32)[:, None]
    col_pos = jnp.arange(NR).astype(jnp.int32)[None, :]
    own_dev = (row_pos // FA) * N_SECTOR + col_pos // FR
    next_dev = (row_pos // FA) * N_SECTOR + (col_pos // FR + 1) % N_SECTOR
    coarse_index = jnp.where(ghost_map < GCELLS, own_dev * GCELLS + ghost_map,
                             next_dev * GCELLS + ghost_map - GCELLS).astype(jnp.int32)
    coarse_at_face = coarse_face[:, :, coarse_index]

    current = fine_populations
    for substep in range(2):
        weight_new = 0.5 * (substep + 1)
        blended = (1.0 - weight_new) * coarse_at_face[0] + weight_new * coarse_at_face[1]
        ghost_pops = interface_values(blended)
        relaxed = collide(current, force_field)
        current = stream(relaxed, ghost_pops)
    return current
```

```python
import functools

import jax
import jax.numpy as jnp
from jax import lax
from jax.experimental import pallas as pl
from jax.experimental.pallas import tpu as pltpu
from jax.sharding import PartitionSpec as P

VELOCITIES = (
    (0, 0, 0),
    (1, 0, 0),
    (-1, 0, 0),
    (0, 1, 0),
    (0, -1, 0),
    (0, 0, 1),
    (0, 0, -1),
    (1, 1, 0),
    (-1, -1, 0),
    (1, -1, 0),
    (-1, 1, 0),
    (1, 0, 1),
    (-1, 0, -1),
    (1, 0, -1),
    (-1, 0, 1),
    (0, 1, 1),
    (0, -1, -1),
    (0, 1, -1),
    (0, -1, 1),
)
LATTICE_WEIGHTS = (1.0 / 3.0,) + (1.0 / 18.0,) * 6 + (1.0 / 36.0,) * 12
TAU_FINE = 0.8
TAU_COARSE = 0.65
FORCE_FACTOR = 1.0 - 0.5 / TAU_FINE
RESCALE = TAU_FINE / (2.0 * TAU_COARSE)

FA, FR, FW = 32, 16, 128
NB, MB = 32, 128
PLANE = 24
OFF = 32
ROWS = OFF + FA * PLANE + PLANE

UP = [i for i in range(19) if VELOCITIES[i][0] == 1]
DOWN = [i for i in range(19) if VELOCITIES[i][0] == -1]
FORTH = [i for i in range(19) if VELOCITIES[i][1] == 1]
BACK = [i for i in range(19) if VELOCITIES[i][1] == -1]
INWARD = [i for i in range(19) if VELOCITIES[i][2] == -1]
ORDER = UP + DOWN + [i for i in range(19) if VELOCITIES[i][0] == 0]
SLOT = {pop: slot for slot, pop in enumerate(ORDER)}

RIM_BACK, RIM_FORTH, GHOST = 0, 1, 2
EXCHANGE = 3
N_REMOTE = EXCHANGE + 16

MESH = pl.DeviceIdType.MESH


def opposite(pop_index):
    if pop_index == 0:
        return 0
    return pop_index + 1 if pop_index % 2 == 1 else pop_index - 1


def collide(f, force, scale):
    gain = -4.0 / scale
    s, d = {}, {}
    for i in range(1, 19, 2):
        s[i] = f[i] + f[i + 1]
        d[i] = f[i] - f[i + 1]
    density = ((f[0] + s[1]) + (s[3] + s[5])) + ((s[7] + s[9]) + (s[11] + s[13])) + (s[15] + s[17])
    momentum = [
        d[1] + (d[7] + d[9]) + (d[11] + d[13]),
        d[3] + (d[7] - d[9]) + (d[15] + d[17]),
        d[5] + (d[11] - d[13]) + (d[15] - d[17]),
    ]
    guess = pl.reciprocal(density, approx=True)
    inverse = guess * (2.0 - density * guess)
    pushed = [momentum[k] + (0.5 / scale) * force[k] for k in range(3)]
    u = [pushed[k] * inverse for k in range(3)]
    h = [(-22.5 / 36.0) * pushed[k] + (gain * 3.375 / 36.0) * force[k] for k in range(3)]
    q = [(-15.0 / 36.0) * pushed[k] + (gain * 1.125 / 36.0) * force[k] for k in range(3)]
    t = [u[k] * h[k] for k in range(3)]
    base = (-5.0 / 36.0) * density - (1.0 / 3.0) * (t[0] + t[1] + t[2])
    out = [None] * 19
    out[0] = f[0] + 12.0 * base
    for k, i in enumerate((1, 3, 5)):
        even = 2.0 * (base + t[k])
        odd = 2.0 * q[k]
        out[i] = f[i] + (even + odd)
        out[i + 1] = f[i + 1] + (even - odd)
    for a, b, i in ((0, 1, 7), (0, 2, 11), (1, 2, 15)):
        common = base + t[a] + t[b]
        cross = u[a] * h[b] + u[b] * h[a]
        for j, even, odd in (
            (i, common + cross, q[a] + q[b]),
            (i + 2, common - cross, q[a] - q[b]),
        ):
            out[j] = f[j] + (even + odd)
            out[j + 1] = f[j + 1] + (even - odd)
    return out


def interface_rows(pops):
    density = pops[0]
    for i in range(1, 19):
        density = density + pops[i]
    velocity = []
    for k in range(3):
        running = jnp.zeros_like(density)
        for i in range(19):
            if VELOCITIES[i][k] == 1:
                running = running + pops[i]
            elif VELOCITIES[i][k] == -1:
                running = running - pops[i]
        velocity.append(running / density)
    speed_sq = velocity[0] * velocity[0] + velocity[1] * velocity[1] + velocity[2] * velocity[2]
    rows = []
    for i in INWARD:
        dotted = jnp.zeros_like(density)
        for k in range(3):
            if VELOCITIES[i][k] == 1:
                dotted = dotted + velocity[k]
            elif VELOCITIES[i][k] == -1:
                dotted = dotted - velocity[k]
        weight = LATTICE_WEIGHTS[i]
        balance = weight * density * (1.0 + 3.0 * dotted + 4.5 * dotted * dotted - 1.5 * speed_sq)
        rows.append(balance + RESCALE * (pops[i] - balance))
    return rows


def pulled(load, ghost, first_column, low, high):
    lane = lax.broadcasted_iota(jnp.int32, (8, FW), 1)
    inner = lane == 0
    outer = lane == FW - 1
    values = []
    for i in range(19):
        ca, cr, cw = VELOCITIES[i]
        value = load(i, -ca, -cr)
        ended = low if ca == 1 else high if ca == -1 else None
        if cw == 1 or ended is not None:
            reflected = load(opposite(i), 0, 0)
        if cw == 1:
            value = jnp.where(inner, reflected, pltpu.roll(value, 1, 1))
        elif cw == -1:
            shift = FW - 1 - (first_column + INWARD.index(i))
            value = jnp.where(outer, pltpu.roll(ghost, shift, 1), pltpu.roll(value, FW - 1, 1))
        if ended is not None:
            value = jnp.where(ended, reflected, value)
        values.append(value)
    return values


def pull_plane(relaxed, ghosts, first_column, a, half, low, high):
    row = OFF + a * PLANE + half * 8

    def load(i, da, dr):
        return relaxed[SLOT[i], pl.ds(row + da * PLANE + dr, 8), :]

    ghost = ghosts[pl.ds(a * FR + half * 8, 8), :]
    return pulled(load, ghost, first_column, low, high)


def pull_rim(relaxed, margin_back, margin_forth, ghosts, first_column, c, r, first, last):
    row = OFF + c * (8 * PLANE) + r

    def load(i, da, dr):
        if r + dr < 0:
            return margin_back[FORTH.index(i), pl.ds(8 + c * 8 + da, 8), :]
        if r + dr >= FR:
            return margin_forth[BACK.index(i), pl.ds(8 + c * 8 + da, 8), :]
        return relaxed[SLOT[i], pl.ds(row + da * PLANE + dr, 8, stride=PLANE), :]

    ghost = ghosts[pl.ds(c * (8 * FR) + r, 8, stride=FR), :]
    along = lax.broadcasted_iota(jnp.int32, (8, FW), 0) + c * 8
    low = along == jnp.where(first, 0, -1)
    high = along == jnp.where(last, FA - 1, -1)
    return pulled(load, ghost, first_column, low, high)


def end_mask(flag):
    return lax.broadcasted_iota(jnp.int32, (8, FW), 0) < jnp.where(flag, 8, 0)


def split(x):
    high = x.astype(jnp.bfloat16)
    rest = x - high.astype(jnp.float32)
    middle = rest.astype(jnp.bfloat16)
    low = (rest - middle.astype(jnp.float32)).astype(jnp.bfloat16)
    return high, middle, low


def advance(
    n_coarse,
    n_sector,
    fine_hbm,
    face_hbm,
    map_hbm,
    mforce_hbm,
    mweights_hbm,
    tiles_hbm,
    count_ref,
    relaxed2,
    back2,
    forth2,
    ghosts,
    fine,
    face,
    gmap,
    mforce,
    mweights,
    tiles_ref,
    rows3,
    parts,
    force,
    rim_back,
    rim_forth,
    gown,
    gnext,
    relaxed1,
    back1,
    forth1,
    sends,
    local_sem,
    send_sem,
    recv_sem,
):
    p = lax.axis_index("coarse")
    s = lax.axis_index("sector")
    ahead = lax.rem(s + 1, n_sector)
    behind = lax.rem(s + n_sector - 1, n_sector)
    first, last = p == 0, p == n_coarse - 1
    has_low, has_high = p > 0, p < n_coarse - 1

    loads = [
        pltpu.make_async_copy(mweights_hbm, mweights, local_sem.at[0]),
        pltpu.make_async_copy(mforce_hbm, mforce, local_sem.at[1]),
        pltpu.make_async_copy(face_hbm, face, local_sem.at[2]),
        pltpu.make_async_copy(map_hbm, gmap, local_sem.at[3]),
        pltpu.make_async_copy(tiles_hbm, tiles_ref, local_sem.at[8]),
    ]
    for c in range(4):
        rows = pl.ds(c * 128, 128)
        loads.append(
            pltpu.make_async_copy(fine_hbm.at[:, rows, :], fine.at[:, rows, :], local_sem.at[4 + c])
        )
    for copy in loads:
        copy.start()

    barrier = pltpu.get_barrier_semaphore()

    def greet(coarse, sector):
        pl.semaphore_signal(
            barrier, inc=1, device_id={"coarse": coarse, "sector": sector}, device_id_type=MESH
        )

    greet(p, ahead)
    greet(p, behind)
    for there, coarse in ((has_low, p - 1), (has_high, p + 1)):

        @pl.when(there)
        def _():
            greet(coarse, s)
            greet(coarse, ahead)
            greet(coarse, behind)

    loads[1].wait()
    for k in range(3):
        rows3[pl.ds(k, NB, stride=8), :] = mforce[k].astype(jnp.float32)
    loads[0].wait()

    def block(b, carry):
        for k in range(4):
            n = b * 4 + k
            rows = pl.ds(pl.multiple_of(n * 8, 8), 8)
            parts[rows, :] = jnp.dot(
                rows3[rows, :].astype(jnp.bfloat16),
                mweights[n],
                preferred_element_type=jnp.float32,
            )
        return carry

    lax.fori_loop(0, NB // 4, block, 0)
    loads[4].wait()
    block_id = lax.rem(lax.broadcasted_iota(jnp.int32, (8, 3 * NB), 1), NB)
    tile = jnp.zeros((8, 3 * NB), jnp.int32)
    for b in range(NB):
        tile = jnp.where(block_id == b, tiles_ref[b], tile)
    axial = lax.shift_right_logical(tile * 3641, 16)
    cycle = tile - axial * (FR + 2)
    target = jnp.where(
        cycle == 0,
        FA * FR + axial,
        jnp.where(cycle == FR + 1, FA * FR + FA + axial, axial * FR + cycle - 1),
    )
    target = jnp.where(block_id < count_ref[0], target, -1)[:1]
    columns = []
    for k in range(3):
        high, middle, low = split(parts[pl.ds(k, NB, stride=8), :])
        columns.append(jnp.concatenate([high, middle, low], axis=0))
    columns = jnp.concatenate(columns, axis=1)
    for n in range(9):
        cell = lax.broadcasted_iota(jnp.int32, (64, 3 * NB), 0) + n * 64
        chosen = jnp.where(cell == target, 1.0, 0.0).astype(jnp.bfloat16)
        summed = jnp.dot(chosen, columns, preferred_element_type=jnp.float32)
        for k in range(3):
            force[k, n * 64 : n * 64 + 64, :] = summed[:, k * FW : k * FW + FW]

    peers = 2 + jnp.where(has_low, 3, 0) + jnp.where(has_high, 3, 0)
    pl.semaphore_wait(barrier, peers)

    def send(n, src, dst, coarse, sector):
        return pltpu.make_async_remote_copy(
            src_ref=src,
            dst_ref=dst,
            send_sem=send_sem.at[n],
            recv_sem=recv_sem.at[n],
            device_id={"coarse": coarse, "sector": sector},
            device_id_type=MESH,
        )

    rims = [
        send(RIM_BACK, force.at[:, 512:544, :], rim_forth, p, behind),
        send(RIM_FORTH, force.at[:, 544:576, :], rim_back, p, ahead),
    ]
    for copy in rims:
        copy.start()

    loads[2].wait()
    for k in range(2):
        new = 0.5 * (k + 1)
        pops = [
            (1.0 - new) * face[i, 0:1, :] + new * face[i, 1:2, :] for i in range(19)
        ]
        for j, row in enumerate(interface_rows(pops)):
            gown[5 * k + j : 5 * k + j + 1, :] = row * (-4.0, 16.0)[k]
    for j in range(10, 16):
        gown[j : j + 1, :] = jnp.zeros((1, FW), jnp.float32)
    ghost_copy = send(GHOST, gown, gnext, p, behind)
    ghost_copy.start()

    def exchange(k, relaxed, back, forth):
        base = EXCHANGE + 8 * k
        top, bottom = OFF + (FA - 1) * PLANE, OFF
        to_back, to_forth = sends.at[2 * k], sends.at[2 * k + 1]
        both = [
            send(base, to_forth, back.at[:, 8:40, :], p, ahead),
            send(base + 1, to_back, forth.at[:, 8:40, :], p, behind),
        ]
        up7, down10 = FORTH.index(7), FORTH.index(10)
        up9, down8 = BACK.index(9), BACK.index(8)
        upward = [
            send(
                base + 2,
                relaxed.at[0:5, top : top + FR, :],
                relaxed.at[0:5, bottom - PLANE : bottom - PLANE + FR, :],
                p + 1,
                s,
            ),
            send(base + 3, to_forth.at[up7, 24:32, :], back.at[up7, 0:8, :], p + 1, ahead),
            send(base + 4, to_back.at[up9, 24:32, :], forth.at[up9, 0:8, :], p + 1, behind),
        ]
        downward = [
            send(
                base + 5,
                relaxed.at[5:10, bottom : bottom + FR, :],
                relaxed.at[5:10, top + PLANE : top + PLANE + FR, :],
                p - 1,
                s,
            ),
            send(base + 6, to_forth.at[down10, 0:8, :], back.at[down10, 40:48, :], p - 1, ahead),
            send(base + 7, to_back.at[down8, 0:8, :], forth.at[down8, 40:48, :], p - 1, behind),
        ]
        return both, upward, downward

    def start(copies):
        both, upward, downward = copies
        for copy in both:
            copy.start()
        for there, group in ((has_high, upward), (has_low, downward)):

            @pl.when(there)
            def _():
                for copy in group:
                    copy.start()

    def arrive(copies):
        both, upward, downward = copies
        for copy in both:
            copy.wait_recv()
        for there, group in ((has_low, upward), (has_high, downward)):

            @pl.when(there)
            def _():
                for copy in group:
                    copy.wait_recv()

    def leave(copies):
        both, upward, downward = copies
        for copy in both:
            copy.wait_send()
        for there, group in ((has_high, upward), (has_low, downward)):

            @pl.when(there)
            def _():
                for copy in group:
                    copy.wait_send()

    def keep_plane(relaxed, a, half, values):
        row = pl.multiple_of(OFF + a * PLANE + half * 8, 8)
        for i in range(19):
            relaxed[SLOT[i], pl.ds(row, 8), :] = values[i]

    def keep_rim(k, relaxed, c, r, values):
        row = OFF + c * (8 * PLANE) + r
        for i in range(19):
            relaxed[SLOT[i], pl.ds(row, 8, stride=PLANE), :] = values[i]
        for j, i in enumerate(BACK if r == 0 else FORTH):
            side = 2 * k if r == 0 else 2 * k + 1
            sends[side, j, pl.ds(pl.multiple_of(c * 8, 8), 8), :] = values[i]

    def plane1(a, carry):
        for half in range(2):
            row = pl.multiple_of(a * FR + half * 8, 8)
            f = [fine[i, pl.ds(row, 8), :] for i in range(19)]
            push = [force[k, pl.ds(row, 8), :] for k in range(3)]
            keep_plane(relaxed1, a, half, collide(f, push, 1.0))
        return carry

    def rim1(c, carry):
        for r, rim in ((0, rim_back), (FR - 1, rim_forth)):
            rows = pl.ds(c * (8 * FR) + r, 8, stride=FR)
            f = [fine[i, rows, :] for i in range(19)]
            along = pl.ds(pl.multiple_of(c * 8, 8), 8)
            push = [force[k, rows, :] + rim[k, along, :] for k in range(3)]
            for k in range(3):
                force[k, rows, :] = push[k]
            keep_rim(0, relaxed1, c, r, collide(f, push, 1.0))
        return carry

    for c in range(4):
        loads[5 + c].wait()
        lax.fori_loop(c * 8, c * 8 + 8, plane1, 0)
    for copy in rims:
        copy.wait_recv()
    lax.fori_loop(0, 4, rim1, 0)
    copies1 = exchange(0, relaxed1, back1, forth1)
    start(copies1)

    loads[3].wait()
    ghost_copy.wait_recv()
    window = jnp.concatenate([gown[...], gnext[...]], axis=1)
    turned = gmap[...]
    cell = lax.broadcasted_iota(jnp.int32, (FR, 2 * FW), 1)
    window_parts = split(window)
    for n in range(4):
        chosen = jnp.concatenate(
            [
                jnp.where(
                    jnp.broadcast_to(turned[:, a : a + 1], (FR, 2 * FW)) == cell, 1.0, 0.0
                )
                for a in range(n * 8, n * 8 + 8)
            ],
            axis=0,
        ).astype(jnp.bfloat16)
        total = jnp.zeros((128, 16), jnp.float32)
        for part in window_parts:
            total = total + lax.dot_general(
                chosen, part, (((1,), (1,)), ((), ())), preferred_element_type=jnp.float32
            )
        ghosts[n * 128 : n * 128 + 128, 0:16] = total

    def plane2(a, low, high):
        for half in range(2):
            f = pull_plane(relaxed1, ghosts, 0, a, half, low, high)
            row = pl.multiple_of(a * FR + half * 8, 8)
            push = [force[k, pl.ds(row, 8), :] for k in range(3)]
            keep_plane(relaxed2, a, half, collide(f, push, -0.25))

    def inner2(a, carry):
        plane2(a, None, None)
        return carry

    def rim2(c, carry):
        for r in (0, FR - 1):
            f = pull_rim(relaxed1, back1, forth1, ghosts, 0, c, r, first, last)
            rows = pl.ds(c * (8 * FR) + r, 8, stride=FR)
            push = [force[k, rows, :] for k in range(3)]
            keep_rim(1, relaxed2, c, r, collide(f, push, -0.25))
        return carry

    lax.fori_loop(1, FA - 1, inner2, 0)
    arrive(copies1)
    plane2(0, end_mask(first), None)
    plane2(FA - 1, None, end_mask(last))
    lax.fori_loop(0, 4, rim2, 0)
    copies2 = exchange(1, relaxed2, back2, forth2)
    start(copies2)
    for copy in rims:
        copy.wait_send()
    ghost_copy.wait_send()
    leave(copies1)
    arrive(copies2)
    leave(copies2)


def settle(n_coarse, relaxed, back, forth, ghosts, out_hbm, out, sem):
    p = lax.axis_index("coarse")
    first, last = p == 0, p == n_coarse - 1

    def plane(a, low, high):
        for half in range(2):
            f = pull_plane(relaxed, ghosts, 5, a, half, low, high)
            row = pl.multiple_of(a * FR + half * 8, 8)
            for i in range(19):
                out[i, pl.ds(row, 8), :] = f[i] * 0.0625

    def inner(a, carry):
        plane(a, None, None)
        return carry

    copies = []
    for c in range(4):
        if c == 0:
            plane(0, end_mask(first), None)
        lax.fori_loop(max(c * 8, 1), min(c * 8 + 8, FA - 1), inner, 0)
        if c == 3:
            plane(FA - 1, None, end_mask(last))
        for r in (0, FR - 1):
            f = pull_rim(relaxed, back, forth, ghosts, 5, c, r, first, last)
            for i in range(19):
                out[i, pl.ds(c * (8 * FR) + r, 8, stride=FR), :] = f[i] * 0.0625
        rows = pl.ds(c * 128, 128)
        copy = pltpu.make_async_copy(out.at[:, rows, :], out_hbm.at[:, rows, :], sem.at[c])
        copy.start()
        copies.append(copy)
    for copy in copies:
        copy.wait()


def local(
    fine_populations,
    coarse_face,
    ghost_map,
    marker_force,
    marker_weights,
    marker_tiles,
    block_counts,
):
    n_coarse, n_sector = lax.axis_size("coarse"), lax.axis_size("sector")
    f32 = jnp.float32
    vmem = pl.BlockSpec(memory_space=pltpu.VMEM)
    hbm = pl.BlockSpec(memory_space=pltpu.HBM)
    margin = (5, 48, FW)
    state = pl.pallas_call(
        functools.partial(advance, n_coarse, n_sector),
        out_shape=(
            pltpu.VMEM((19, ROWS, FW), f32),
            pltpu.VMEM(margin, f32),
            pltpu.VMEM(margin, f32),
            pltpu.VMEM((FA * FR, FW), f32),
        ),
        in_specs=[hbm] * 6 + [pl.BlockSpec(memory_space=pltpu.SMEM)],
        out_specs=(vmem, vmem, vmem, vmem),
        scratch_shapes=[
            pltpu.VMEM((19, FA * FR, FW), f32),
            pltpu.VMEM((19, 2, FW), f32),
            pltpu.VMEM((FR, FA), jnp.int32),
            pltpu.VMEM((3, NB, MB), jnp.bfloat16),
            pltpu.VMEM((NB, MB, FW), jnp.bfloat16),
            pltpu.SMEM((NB,), jnp.int32),
            pltpu.VMEM((NB * 8, MB), f32),
            pltpu.VMEM((NB * 8, FW), f32),
            pltpu.VMEM((3, FA * FR + 2 * FA, FW), f32),
            pltpu.VMEM((3, FA, FW), f32),
            pltpu.VMEM((3, FA, FW), f32),
            pltpu.VMEM((16, FW), f32),
            pltpu.VMEM((16, FW), f32),
            pltpu.VMEM((19, ROWS, FW), f32),
            pltpu.VMEM(margin, f32),
            pltpu.VMEM(margin, f32),
            pltpu.VMEM((4, 5, FA, FW), f32),
            pltpu.SemaphoreType.DMA((9,)),
            pltpu.SemaphoreType.DMA((N_REMOTE,)),
            pltpu.SemaphoreType.DMA((N_REMOTE,)),
        ],
        compiler_params=pltpu.CompilerParams(
            collective_id=0, has_side_effects=True, vmem_limit_bytes=32 * 1024 * 1024
        ),
        name="advance",
    )(
        *(
            pltpu.with_memory_space_constraint(x, pltpu.HBM)
            for x in (
                fine_populations.reshape(19, FA * FR, FW),
                jnp.transpose(coarse_face, (1, 0, 2)),
                jnp.transpose(ghost_map),
                jnp.transpose(marker_force, (1, 0, 2)),
                marker_weights,
                marker_tiles,
            )
        ),
        block_counts,
    )
    out = pl.pallas_call(
        functools.partial(settle, n_coarse),
        out_shape=jax.ShapeDtypeStruct((19, FA * FR, FW), f32),
        in_specs=[vmem, vmem, vmem, vmem],
        out_specs=hbm,
        scratch_shapes=[
            pltpu.VMEM((19, FA * FR, FW), f32),
            pltpu.SemaphoreType.DMA((4,)),
        ],
        compiler_params=pltpu.CompilerParams(vmem_limit_bytes=32 * 1024 * 1024),
        name="settle",
    )(*state)
    return out.reshape(19, FA, FR, FW)


def solution(mesh):
    in_specs = (
        P(None, "coarse", "sector", None),
        P(None, None, ("coarse", "sector")),
        P("coarse", "sector"),
        P(("coarse", "sector"), None, None),
        P(("coarse", "sector"), None, None),
        P(("coarse", "sector")),
        P(("coarse", "sector")),
    )
    out_specs = P(None, "coarse", "sector", None)
    return jax.shard_map(local, mesh=mesh, in_specs=in_specs, out_specs=out_specs, check_vma=False)
```

```python
import functools

import jax
import jax.numpy as jnp
from jax import lax
from jax.experimental import pallas as pl
from jax.experimental.pallas import tpu as pltpu
from jax.sharding import PartitionSpec as P

VELOCITIES = (
    (0, 0, 0),
    (1, 0, 0),
    (-1, 0, 0),
    (0, 1, 0),
    (0, -1, 0),
    (0, 0, 1),
    (0, 0, -1),
    (1, 1, 0),
    (-1, -1, 0),
    (1, -1, 0),
    (-1, 1, 0),
    (1, 0, 1),
    (-1, 0, -1),
    (1, 0, -1),
    (-1, 0, 1),
    (0, 1, 1),
    (0, -1, -1),
    (0, 1, -1),
    (0, -1, 1),
)
LATTICE_WEIGHTS = (1.0 / 3.0,) + (1.0 / 18.0,) * 6 + (1.0 / 36.0,) * 12
TAU_FINE = 0.8
TAU_COARSE = 0.65
FORCE_FACTOR = 1.0 - 0.5 / TAU_FINE
RESCALE = TAU_FINE / (2.0 * TAU_COARSE)

FA, FR, FW = 32, 16, 128
NB, MB = 32, 128
PLANE = 24
OFF = 32
ROWS = OFF + FA * PLANE + PLANE

UP = [i for i in range(19) if VELOCITIES[i][0] == 1]
DOWN = [i for i in range(19) if VELOCITIES[i][0] == -1]
FORTH = [3, 15, 17, 10, 7]
BACK = [4, 16, 18, 8, 9]
INWARD = [i for i in range(19) if VELOCITIES[i][2] == -1]
ORDER = UP + DOWN + [i for i in range(19) if VELOCITIES[i][0] == 0]
SLOT = {pop: slot for slot, pop in enumerate(ORDER)}

V_AT, INVERSE_AT, RIM_AT, PARTS = 5, 8, 9, 12

GHOST, FIRST, SECOND = 0, 1, 13
N_REMOTE = SECOND + 8

MESH = pl.DeviceIdType.MESH


def opposite(pop_index):
    if pop_index == 0:
        return 0
    return pop_index + 1 if pop_index % 2 == 1 else pop_index - 1


def collide(f, force, scale):
    gain = -4.0 / scale
    s, d = {}, {}
    for i in range(1, 19, 2):
        s[i] = f[i] + f[i + 1]
        d[i] = f[i] - f[i + 1]
    density = ((f[0] + s[1]) + (s[3] + s[5])) + ((s[7] + s[9]) + (s[11] + s[13])) + (s[15] + s[17])
    momentum = [
        d[1] + (d[7] + d[9]) + (d[11] + d[13]),
        d[3] + (d[7] - d[9]) + (d[15] + d[17]),
        d[5] + (d[11] - d[13]) + (d[15] - d[17]),
    ]
    guess = pl.reciprocal(density, approx=True)
    inverse = guess * (2.0 - density * guess)
    pushed = [momentum[k] + (0.5 / scale) * force[k] for k in range(3)]
    u = [pushed[k] * inverse for k in range(3)]
    h = [(-22.5 / 36.0) * pushed[k] + (gain * 3.375 / 36.0) * force[k] for k in range(3)]
    q = [(-15.0 / 36.0) * pushed[k] + (gain * 1.125 / 36.0) * force[k] for k in range(3)]
    t = [u[k] * h[k] for k in range(3)]
    base = (-5.0 / 36.0) * density - (1.0 / 3.0) * (t[0] + t[1] + t[2])
    out = [None] * 19
    out[0] = f[0] + 12.0 * base
    for k, i in enumerate((1, 3, 5)):
        even = 2.0 * (base + t[k])
        odd = 2.0 * q[k]
        out[i] = f[i] + (even + odd)
        out[i + 1] = f[i + 1] + (even - odd)
    for a, b, i in ((0, 1, 7), (0, 2, 11), (1, 2, 15)):
        common = base + t[a] + t[b]
        cross = u[a] * h[b] + u[b] * h[a]
        for j, even, odd in (
            (i, common + cross, q[a] + q[b]),
            (i + 2, common - cross, q[a] - q[b]),
        ):
            out[j] = f[j] + (even + odd)
            out[j + 1] = f[j + 1] + (even - odd)
    return out, u, inverse


def along(vector, i):
    terms = [vector[k] if VELOCITIES[i][k] == 1 else -vector[k] for k in range(3) if VELOCITIES[i][k]]
    return functools.reduce(lambda x, y: x + y, terms)


def corrected(base, pops, extra, v, inverse):
    w = [v[k] + 1.03125 * inverse * extra[k] for k in range(3)]
    shared = w[0] * extra[0] + w[1] * extra[1] + w[2] * extra[2]
    values = []
    for value, i in zip(base, pops):
        pushed = along(extra, i)
        grown = 3.0 * (pushed + along(w, i) * pushed) - shared
        values.append(value - (4.0 * LATTICE_WEIGHTS[i]) * grown)
    return values


def interface_rows(pops):
    density = pops[0]
    for i in range(1, 19):
        density = density + pops[i]
    velocity = []
    for k in range(3):
        running = jnp.zeros_like(density)
        for i in range(19):
            if VELOCITIES[i][k] == 1:
                running = running + pops[i]
            elif VELOCITIES[i][k] == -1:
                running = running - pops[i]
        velocity.append(running / density)
    speed_sq = velocity[0] * velocity[0] + velocity[1] * velocity[1] + velocity[2] * velocity[2]
    rows = []
    for i in INWARD:
        dotted = jnp.zeros_like(density)
        for k in range(3):
            if VELOCITIES[i][k] == 1:
                dotted = dotted + velocity[k]
            elif VELOCITIES[i][k] == -1:
                dotted = dotted - velocity[k]
        weight = LATTICE_WEIGHTS[i]
        balance = weight * density * (1.0 + 3.0 * dotted + 4.5 * dotted * dotted - 1.5 * speed_sq)
        rows.append(balance + RESCALE * (pops[i] - balance))
    return rows


def pulled(load, ghost, first_column, low, high):
    lane = lax.broadcasted_iota(jnp.int32, (8, FW), 1)
    inner = lane == 0
    outer = lane == FW - 1
    values = []
    for i in range(19):
        ca, cr, cw = VELOCITIES[i]
        value = load(i, -ca, -cr)
        ended = low if ca == 1 else high if ca == -1 else None
        if cw == 1 or ended is not None:
            reflected = load(opposite(i), 0, 0)
        if cw == 1:
            value = jnp.where(inner, reflected, pltpu.roll(value, 1, 1))
        elif cw == -1:
            shift = FW - 1 - (first_column + INWARD.index(i))
            value = jnp.where(outer, pltpu.roll(ghost, shift, 1), pltpu.roll(value, FW - 1, 1))
        if ended is not None:
            value = jnp.where(ended, reflected, value)
        values.append(value)
    return values


def pull_plane(relaxed, ghosts, first_column, a, half, low, high):
    row = OFF + a * PLANE + half * 8

    def load(i, da, dr):
        return relaxed[SLOT[i], pl.ds(row + da * PLANE + dr, 8), :]

    ghost = ghosts[pl.ds(a * FR + half * 8, 8), :]
    return pulled(load, ghost, first_column, low, high)


def pull_rim(relaxed, margin, ghosts, first_column, c, r, first, last):
    row = OFF + c * (8 * PLANE) + r

    def load(i, da, dr):
        if r + dr < 0:
            return margin[0, FORTH.index(i), pl.ds(8 + c * 8 + da, 8), :]
        if r + dr >= FR:
            return margin[1, BACK.index(i), pl.ds(8 + c * 8 + da, 8), :]
        return relaxed[SLOT[i], pl.ds(row + da * PLANE + dr, 8, stride=PLANE), :]

    ghost = ghosts[pl.ds(c * (8 * FR) + r, 8, stride=FR), :]
    axial = lax.broadcasted_iota(jnp.int32, (8, FW), 0) + c * 8
    low = axial == jnp.where(first, 0, -1)
    high = axial == jnp.where(last, FA - 1, -1)
    return pulled(load, ghost, first_column, low, high)


def end_mask(flag):
    return lax.broadcasted_iota(jnp.int32, (8, FW), 0) < jnp.where(flag, 8, 0)


def split(x):
    high = x.astype(jnp.bfloat16)
    rest = x - high.astype(jnp.float32)
    middle = rest.astype(jnp.bfloat16)
    low = (rest - middle.astype(jnp.float32)).astype(jnp.bfloat16)
    return high, middle, low


def advance(
    n_coarse,
    n_sector,
    fine_hbm,
    face_hbm,
    map_hbm,
    mforce_hbm,
    mweights_hbm,
    tiles_hbm,
    count_ref,
    relaxed2,
    margin2,
    ghosts,
    fine,
    face,
    gmap,
    mforce,
    mweights,
    tiles_ref,
    rows3,
    parts,
    force,
    rims,
    gown,
    gnext,
    relaxed1,
    margin1,
    outbox,
    inbox,
    edges,
    sends,
    local_sem,
    send_sem,
    recv_sem,
):
    p = lax.axis_index("coarse")
    s = lax.axis_index("sector")
    ahead = lax.rem(s + 1, n_sector)
    behind = lax.rem(s + n_sector - 1, n_sector)
    first, last = p == 0, p == n_coarse - 1
    has_low, has_high = p > 0, p < n_coarse - 1

    loads = [
        pltpu.make_async_copy(mweights_hbm, mweights, local_sem.at[0]),
        pltpu.make_async_copy(mforce_hbm, mforce, local_sem.at[1]),
        pltpu.make_async_copy(face_hbm, face, local_sem.at[2]),
        pltpu.make_async_copy(map_hbm, gmap, local_sem.at[3]),
        pltpu.make_async_copy(tiles_hbm, tiles_ref, local_sem.at[8]),
    ]
    for c in range(4):
        rows = pl.ds(c * 128, 128)
        loads.append(
            pltpu.make_async_copy(fine_hbm.at[:, rows, :], fine.at[:, rows, :], local_sem.at[4 + c])
        )
    for copy in loads:
        copy.start()

    barrier = pltpu.get_barrier_semaphore()

    def greet(coarse, sector):
        pl.semaphore_signal(
            barrier, inc=1, device_id={"coarse": coarse, "sector": sector}, device_id_type=MESH
        )

    greet(p, ahead)
    greet(p, behind)
    for there, coarse in ((has_low, p - 1), (has_high, p + 1)):

        @pl.when(there)
        def _():
            greet(coarse, s)
            greet(coarse, ahead)
            greet(coarse, behind)

    loads[1].wait()
    for k in range(3):
        rows3[pl.ds(k, NB, stride=8), :] = mforce[k].astype(jnp.float32)
    loads[0].wait()

    def block(b, carry):
        for k in range(4):
            n = b * 4 + k
            rows = pl.ds(pl.multiple_of(n * 8, 8), 8)
            parts[rows, :] = jnp.dot(
                rows3[rows, :].astype(jnp.bfloat16),
                mweights[n],
                preferred_element_type=jnp.float32,
            )
        return carry

    lax.fori_loop(0, NB // 4, block, 0)
    loads[4].wait()
    block_id = lax.rem(lax.broadcasted_iota(jnp.int32, (8, 3 * NB), 1), NB)
    tile = jnp.zeros((8, 3 * NB), jnp.int32)
    for b in range(NB):
        tile = jnp.where(block_id == b, tiles_ref[b], tile)
    axial = lax.shift_right_logical(tile * 3641, 16)
    cycle = tile - axial * (FR + 2)
    target = jnp.where(
        cycle == 0,
        FA * FR + axial,
        jnp.where(cycle == FR + 1, FA * FR + FA + axial, axial * FR + cycle - 1),
    )
    target = jnp.where(block_id < count_ref[0], target, -1)[:1]
    columns = []
    for k in range(3):
        high, middle, low = split(parts[pl.ds(k, NB, stride=8), :])
        columns.append(jnp.concatenate([high, middle, low], axis=0))
    columns = jnp.concatenate(columns, axis=1)
    for n in range(9):
        cell = lax.broadcasted_iota(jnp.int32, (64, 3 * NB), 0) + n * 64
        chosen = jnp.where(cell == target, 1.0, 0.0).astype(jnp.bfloat16)
        summed = jnp.dot(chosen, columns, preferred_element_type=jnp.float32)
        for k in range(3):
            column = summed[:, k * FW : k * FW + FW]
            if n < 8:
                force[k, n * 64 : n * 64 + 64, :] = column
            else:
                for side in range(2):
                    rim = column[side * FA : side * FA + FA]
                    rims[side, k, 8:40, :] = rim
                    outbox[side, RIM_AT + k, :, :] = rim

    def send(n, src, dst, coarse, sector):
        return pltpu.make_async_remote_copy(
            src_ref=src,
            dst_ref=dst,
            send_sem=send_sem.at[n],
            recv_sem=recv_sem.at[n],
            device_id={"coarse": coarse, "sector": sector},
            device_id_type=MESH,
        )

    loads[2].wait()
    for k in range(2):
        new = 0.5 * (k + 1)
        pops = [
            (1.0 - new) * face[i, 0:1, :] + new * face[i, 1:2, :] for i in range(19)
        ]
        for j, row in enumerate(interface_rows(pops)):
            gown[5 * k + j : 5 * k + j + 1, :] = row * (-4.0, 16.0)[k]
    for j in range(10, 16):
        gown[j : j + 1, :] = jnp.zeros((1, FW), jnp.float32)
    ghost_copy = send(GHOST, gown, gnext, p, behind)
    top, bottom = OFF + (FA - 1) * PLANE, OFF

    def planes(n, relaxed):
        upward = send(
            n,
            relaxed.at[0:5, top : top + FR, :],
            relaxed.at[0:5, bottom - PLANE : bottom - PLANE + FR, :],
            p + 1,
            s,
        )
        downward = send(
            n + 1,
            relaxed.at[5:10, bottom : bottom + FR, :],
            relaxed.at[5:10, top + PLANE : top + PLANE + FR, :],
            p - 1,
            s,
        )
        return upward, downward

    def first_exchange():
        n = FIRST
        both = [
            send(n, outbox.at[1], inbox.at[0, :, 8:40, :], p, ahead),
            send(n + 1, outbox.at[0], inbox.at[1, :, 8:40, :], p, behind),
        ]
        upward, downward = planes(n + 2, relaxed1)
        upward, downward = [upward], [downward]
        for group, m, coarse, low, there, edge in (
            (upward, n + 4, p + 1, 24, 0, 0),
            (downward, n + 8, p - 1, 0, 40, 1),
        ):
            group += [
                send(
                    m,
                    rims.at[:, :, 8 + low : 16 + low, :],
                    rims.at[:, :, there : there + 8, :],
                    coarse,
                    s,
                ),
                send(
                    m + 1,
                    outbox.at[:, V_AT:RIM_AT, low : low + 8, :],
                    edges.at[edge],
                    coarse,
                    s,
                ),
                send(
                    m + 2,
                    outbox.at[1, 3:PARTS, low : low + 8, :],
                    inbox.at[0, 3:PARTS, there : there + 8, :],
                    coarse,
                    ahead,
                ),
                send(
                    m + 3,
                    outbox.at[0, 3:PARTS, low : low + 8, :],
                    inbox.at[1, 3:PARTS, there : there + 8, :],
                    coarse,
                    behind,
                ),
            ]
        return both, upward, downward

    def second_exchange():
        n = SECOND
        both = [
            send(n, sends.at[1], margin2.at[0, :, 8:40, :], p, ahead),
            send(n + 1, sends.at[0], margin2.at[1, :, 8:40, :], p, behind),
        ]
        upward, downward = planes(n + 2, relaxed2)
        upward = [
            upward,
            send(n + 4, sends.at[1, 4, 24:32, :], margin2.at[0, 4, 0:8, :], p + 1, ahead),
            send(n + 5, sends.at[0, 4, 24:32, :], margin2.at[1, 4, 0:8, :], p + 1, behind),
        ]
        downward = [
            downward,
            send(n + 6, sends.at[1, 3, 0:8, :], margin2.at[0, 3, 40:48, :], p - 1, ahead),
            send(n + 7, sends.at[0, 3, 0:8, :], margin2.at[1, 3, 40:48, :], p - 1, behind),
        ]
        return both, upward, downward

    def start(copies):
        both, upward, downward = copies
        for copy in both:
            copy.start()
        for there, group in ((has_high, upward), (has_low, downward)):

            @pl.when(there)
            def _():
                for copy in group:
                    copy.start()

    def arrive(copies):
        both, upward, downward = copies
        for copy in both:
            copy.wait_recv()
        for there, group in ((has_low, upward), (has_high, downward)):

            @pl.when(there)
            def _():
                for copy in group:
                    copy.wait_recv()

    def leave(copies):
        both, upward, downward = copies
        for copy in both:
            copy.wait_send()
        for there, group in ((has_high, upward), (has_low, downward)):

            @pl.when(there)
            def _():
                for copy in group:
                    copy.wait_send()

    def keep_plane(relaxed, a, half, values, inside=False):
        rows = pl.ds(pl.multiple_of(OFF + a * PLANE + half * 8, 8), 8)
        for i in range(19):
            if inside:
                row = lax.broadcasted_iota(jnp.int32, (8, FW), 0)
                pltpu.store(relaxed.at[SLOT[i], rows, :], values[i], mask=row != 7 * half)
            else:
                relaxed[SLOT[i], rows, :] = values[i]

    def plane1(a, carry):
        for half in range(2):
            row = pl.multiple_of(a * FR + half * 8, 8)
            f = [fine[i, pl.ds(row, 8), :] for i in range(19)]
            push = [force[k, pl.ds(row, 8), :] for k in range(3)]
            keep_plane(relaxed1, a, half, collide(f, push, 1.0)[0])
        return carry

    def rim0(c):
        for side, r in ((0, 0), (1, FR - 1)):
            rows = pl.ds(c * (8 * FR) + r, 8, stride=FR)
            f = [fine[i, rows, :] for i in range(19)]
            push = [force[k, rows, :] for k in range(3)]
            values, u, inverse = collide(f, push, 1.0)
            cells = slice(c * 8, c * 8 + 8)
            for j, i in enumerate(FORTH if side else BACK):
                outbox[side, j, cells, :] = values[i]
            for k in range(3):
                outbox[side, V_AT + k, cells, :] = 3.0 * u[k] + 0.5625 * inverse * push[k]
            outbox[side, INVERSE_AT, cells, :] = inverse

    for c in range(4):
        loads[5 + c].wait()
        rim0(c)
    plane1(0, 0)
    plane1(FA - 1, 0)

    peers = 2 + jnp.where(has_low, 3, 0) + jnp.where(has_high, 3, 0)
    pl.semaphore_wait(barrier, peers)
    ghost_copy.start()
    copies1 = first_exchange()
    start(copies1)
    lax.fori_loop(1, FA - 1, plane1, 0, unroll=2)

    loads[3].wait()
    ghost_copy.wait_recv()
    window = jnp.concatenate([gown[...], gnext[...]], axis=1)
    turned = gmap[...]
    cell = lax.broadcasted_iota(jnp.int32, (FR, 2 * FW), 1)
    window_parts = split(window)
    for n in range(4):
        chosen = jnp.concatenate(
            [
                jnp.where(
                    jnp.broadcast_to(turned[:, a : a + 1], (FR, 2 * FW)) == cell, 1.0, 0.0
                )
                for a in range(n * 8, n * 8 + 8)
            ],
            axis=0,
        ).astype(jnp.bfloat16)
        total = jnp.zeros((128, 16), jnp.float32)
        for part in window_parts:
            total = total + lax.dot_general(
                chosen, part, (((1,), (1,)), ((), ())), preferred_element_type=jnp.float32
            )
        ghosts[n * 128 : n * 128 + 128, 0:16] = total

    def plane2(a, low, high, inside=False):
        for half in range(2):
            f = pull_plane(relaxed1, ghosts, 0, a, half, low, high)
            row = pl.multiple_of(a * FR + half * 8, 8)
            push = [force[k, pl.ds(row, 8), :] for k in range(3)]
            keep_plane(relaxed2, a, half, collide(f, push, -0.25)[0], inside)

    def inner2(a, carry):
        plane2(a, None, None, inside=True)
        return carry

    def keep_rim(relaxed, c, r, values):
        row = OFF + c * (8 * PLANE) + r
        for i in range(19):
            relaxed[SLOT[i], pl.ds(row, 8, stride=PLANE), :] = values[i]

    def rim1(c):
        for side, r in ((0, 0), (1, FR - 1)):
            rows = pl.ds(c * (8 * FR) + r, 8, stride=FR)
            f = [fine[i, rows, :] for i in range(19)]
            cells = slice(8 + c * 8, 16 + c * 8)
            push = [force[k, rows, :] + inbox[side, RIM_AT + k, cells, :] for k in range(3)]
            for k in range(3):
                force[k, rows, :] = push[k]
            keep_rim(relaxed1, c, r, collide(f, push, 1.0)[0])

    def rim2(c):
        for side, r in ((0, 0), (1, FR - 1)):
            f = pull_rim(relaxed1, margin1, ghosts, 0, c, r, first, last)
            rows = pl.ds(c * (8 * FR) + r, 8, stride=FR)
            push = [force[k, rows, :] for k in range(3)]
            values = collide(f, push, -0.25)[0]
            keep_rim(relaxed2, c, r, values)
            for j, i in enumerate(FORTH if side else BACK):
                sends[side, j, c * 8 : c * 8 + 8, :] = values[i]

    arrive(copies1)
    leave(copies1)
    for c in range(4):
        rim1(c)
    for side in range(2):
        for c in range(6):
            cells = slice(c * 8, c * 8 + 8)
            values = corrected(
                [inbox[side, j, cells, :] for j in range(5)],
                BACK if side else FORTH,
                [rims[side, k, cells, :] for k in range(3)],
                [inbox[side, V_AT + k, cells, :] for k in range(3)],
                inbox[side, INVERSE_AT, cells, :],
            )
            for j in range(5):
                margin1[side, j, cells, :] = values[j]
    for edge, pops, plane, at, near in ((0, UP, -1, 7, 7), (1, DOWN, FA, 40, 0)):
        for side, r in ((0, 0), (1, FR - 1)):
            row = OFF + plane * PLANE + r
            values = corrected(
                [relaxed1[SLOT[i], row : row + 1, :] for i in pops],
                pops,
                [inbox[side, RIM_AT + k, at : at + 1, :] for k in range(3)],
                [edges[edge, side, k, near : near + 1, :] for k in range(3)],
                edges[edge, side, 3, near : near + 1, :],
            )
            for i, value in zip(pops, values):
                relaxed1[SLOT[i], row : row + 1, :] = value
    plane2(0, end_mask(first), None)
    plane2(FA - 1, None, end_mask(last))
    for c in range(4):
        rim2(c)
    copies2 = second_exchange()
    start(copies2)
    lax.fori_loop(1, FA - 1, inner2, 0, unroll=5)
    ghost_copy.wait_send()
    arrive(copies2)
    leave(copies2)


def settle(n_coarse, relaxed, margin, ghosts, out_hbm, out, sem):
    p = lax.axis_index("coarse")
    first, last = p == 0, p == n_coarse - 1

    def plane(a, low, high):
        for half in range(2):
            f = pull_plane(relaxed, ghosts, 5, a, half, low, high)
            row = pl.multiple_of(a * FR + half * 8, 8)
            for i in range(19):
                out[i, pl.ds(row, 8), :] = f[i] * 0.0625

    def inner(a, carry):
        plane(a, None, None)
        return carry

    copies = []
    for c in range(4):
        if c == 0:
            plane(0, end_mask(first), None)
        lax.fori_loop(max(c * 8, 1), min(c * 8 + 8, FA - 1), inner, 0, unroll=True)
        if c == 3:
            plane(FA - 1, None, end_mask(last))
        for r in (0, FR - 1):
            f = pull_rim(relaxed, margin, ghosts, 5, c, r, first, last)
            for i in range(19):
                out[i, pl.ds(c * (8 * FR) + r, 8, stride=FR), :] = f[i] * 0.0625
        rows = pl.ds(c * 128, 128)
        copy = pltpu.make_async_copy(out.at[:, rows, :], out_hbm.at[:, rows, :], sem.at[c])
        copy.start()
        copies.append(copy)
    for copy in copies:
        copy.wait()


def local(
    fine_populations,
    coarse_face,
    ghost_map,
    marker_force,
    marker_weights,
    marker_tiles,
    block_counts,
):
    n_coarse, n_sector = lax.axis_size("coarse"), lax.axis_size("sector")
    f32 = jnp.float32
    vmem = pl.BlockSpec(memory_space=pltpu.VMEM)
    hbm = pl.BlockSpec(memory_space=pltpu.HBM)
    margin = (2, 5, 48, FW)
    state = pl.pallas_call(
        functools.partial(advance, n_coarse, n_sector),
        out_shape=(
            pltpu.VMEM((19, ROWS, FW), f32),
            pltpu.VMEM(margin, f32),
            pltpu.VMEM((FA * FR, FW), f32),
        ),
        in_specs=[hbm] * 6 + [pl.BlockSpec(memory_space=pltpu.SMEM)],
        out_specs=(vmem, vmem, vmem),
        scratch_shapes=[
            pltpu.VMEM((19, FA * FR, FW), f32),
            pltpu.VMEM((19, 2, FW), f32),
            pltpu.VMEM((FR, FA), jnp.int32),
            pltpu.VMEM((3, NB, MB), jnp.bfloat16),
            pltpu.VMEM((NB, MB, FW), jnp.bfloat16),
            pltpu.SMEM((NB,), jnp.int32),
            pltpu.VMEM((NB * 8, MB), f32),
            pltpu.VMEM((NB * 8, FW), f32),
            pltpu.VMEM((3, FA * FR, FW), f32),
            pltpu.VMEM((2, 3, 48, FW), f32),
            pltpu.VMEM((16, FW), f32),
            pltpu.VMEM((16, FW), f32),
            pltpu.VMEM((19, ROWS, FW), f32),
            pltpu.VMEM(margin, f32),
            pltpu.VMEM((2, PARTS, FA, FW), f32),
            pltpu.VMEM((2, PARTS, 48, FW), f32),
            pltpu.VMEM((2, 2, 4, 8, FW), f32),
            pltpu.VMEM((2, 5, FA, FW), f32),
            pltpu.SemaphoreType.DMA((9,)),
            pltpu.SemaphoreType.DMA((N_REMOTE,)),
            pltpu.SemaphoreType.DMA((N_REMOTE,)),
        ],
        compiler_params=pltpu.CompilerParams(
            collective_id=0, has_side_effects=True, vmem_limit_bytes=32 * 1024 * 1024
        ),
        name="advance",
    )(
        *(
            pltpu.with_memory_space_constraint(x, pltpu.HBM)
            for x in (
                fine_populations.reshape(19, FA * FR, FW),
                jnp.transpose(coarse_face, (1, 0, 2)),
                jnp.transpose(ghost_map),
                jnp.transpose(marker_force, (1, 0, 2)),
                marker_weights,
                marker_tiles,
            )
        ),
        block_counts,
    )
    out = pl.pallas_call(
        functools.partial(settle, n_coarse),
        out_shape=jax.ShapeDtypeStruct((19, FA * FR, FW), f32),
        in_specs=[vmem, vmem, vmem],
        out_specs=hbm,
        scratch_shapes=[
            pltpu.VMEM((19, FA * FR, FW), f32),
            pltpu.SemaphoreType.DMA((4,)),
        ],
        compiler_params=pltpu.CompilerParams(vmem_limit_bytes=32 * 1024 * 1024),
        name="settle",
    )(*state)
    return out.reshape(19, FA, FR, FW)


def solution(mesh):
    in_specs = (
        P(None, "coarse", "sector", None),
        P(None, None, ("coarse", "sector")),
        P("coarse", "sector"),
        P(("coarse", "sector"), None, None),
        P(("coarse", "sector"), None, None),
        P(("coarse", "sector")),
        P(("coarse", "sector")),
    )
    out_specs = P(None, "coarse", "sector", None)
    return jax.shard_map(local, mesh=mesh, in_specs=in_specs, out_specs=out_specs, check_vma=False)
```

```python
import functools

import jax
import jax.numpy as jnp
from jax import lax
from jax.experimental import pallas as pl
from jax.experimental.pallas import tpu as pltpu
from jax.sharding import PartitionSpec as P

VELOCITIES = (
    (0, 0, 0),
    (1, 0, 0),
    (-1, 0, 0),
    (0, 1, 0),
    (0, -1, 0),
    (0, 0, 1),
    (0, 0, -1),
    (1, 1, 0),
    (-1, -1, 0),
    (1, -1, 0),
    (-1, 1, 0),
    (1, 0, 1),
    (-1, 0, -1),
    (1, 0, -1),
    (-1, 0, 1),
    (0, 1, 1),
    (0, -1, -1),
    (0, 1, -1),
    (0, -1, 1),
)
LATTICE_WEIGHTS = (1.0 / 3.0,) + (1.0 / 18.0,) * 6 + (1.0 / 36.0,) * 12
TAU_FINE = 0.8
TAU_COARSE = 0.65
FORCE_FACTOR = 1.0 - 0.5 / TAU_FINE
RESCALE = TAU_FINE / (2.0 * TAU_COARSE)

FA, FR, FW = 32, 16, 128
NB, MB = 32, 128
PLANE = 24
OFF = 32
ROWS = OFF + FA * PLANE + PLANE

UP = [i for i in range(19) if VELOCITIES[i][0] == 1]
DOWN = [i for i in range(19) if VELOCITIES[i][0] == -1]
FORTH = [3, 15, 17, 10, 7]
BACK = [4, 16, 18, 8, 9]
INWARD = [i for i in range(19) if VELOCITIES[i][2] == -1]
ORDER = UP + DOWN + [i for i in range(19) if VELOCITIES[i][0] == 0]
SLOT = {pop: slot for slot, pop in enumerate(ORDER)}

V_AT, INVERSE_AT, RIM_AT, PARTS = 5, 8, 9, 12

GHOST, FIRST, SECOND = 0, 1, 19
N_REMOTE = SECOND + 14
CHUNKS = 4

MESH = pl.DeviceIdType.MESH


def opposite(pop_index):
    if pop_index == 0:
        return 0
    return pop_index + 1 if pop_index % 2 == 1 else pop_index - 1


def collide(f, force, scale):
    gain = -4.0 / scale
    s, d = {}, {}
    for i in range(1, 19, 2):
        s[i] = f[i] + f[i + 1]
        d[i] = f[i] - f[i + 1]
    density = ((f[0] + s[1]) + (s[3] + s[5])) + ((s[7] + s[9]) + (s[11] + s[13])) + (s[15] + s[17])
    momentum = [
        d[1] + (d[7] + d[9]) + (d[11] + d[13]),
        d[3] + (d[7] - d[9]) + (d[15] + d[17]),
        d[5] + (d[11] - d[13]) + (d[15] - d[17]),
    ]
    guess = pl.reciprocal(density, approx=True)
    inverse = guess * (2.0 - density * guess)
    pushed = [momentum[k] + (0.5 / scale) * force[k] for k in range(3)]
    u = [pushed[k] * inverse for k in range(3)]
    h = [(-22.5 / 36.0) * pushed[k] + (gain * 3.375 / 36.0) * force[k] for k in range(3)]
    q = [(-15.0 / 36.0) * pushed[k] + (gain * 1.125 / 36.0) * force[k] for k in range(3)]
    t = [u[k] * h[k] for k in range(3)]
    base = (-5.0 / 36.0) * density - (1.0 / 3.0) * (t[0] + t[1] + t[2])
    out = [None] * 19
    out[0] = f[0] + 12.0 * base
    for k, i in enumerate((1, 3, 5)):
        even = 2.0 * (base + t[k])
        odd = 2.0 * q[k]
        out[i] = f[i] + (even + odd)
        out[i + 1] = f[i + 1] + (even - odd)
    for a, b, i in ((0, 1, 7), (0, 2, 11), (1, 2, 15)):
        common = base + t[a] + t[b]
        cross = u[a] * h[b] + u[b] * h[a]
        for j, even, odd in (
            (i, common + cross, q[a] + q[b]),
            (i + 2, common - cross, q[a] - q[b]),
        ):
            out[j] = f[j] + (even + odd)
            out[j + 1] = f[j + 1] + (even - odd)
    return out, u, inverse


def along(vector, i):
    terms = [vector[k] if VELOCITIES[i][k] == 1 else -vector[k] for k in range(3) if VELOCITIES[i][k]]
    return functools.reduce(lambda x, y: x + y, terms)


def corrected(base, pops, extra, v, inverse):
    w = [v[k] + 1.03125 * inverse * extra[k] for k in range(3)]
    shared = w[0] * extra[0] + w[1] * extra[1] + w[2] * extra[2]
    values = []
    for value, i in zip(base, pops):
        pushed = along(extra, i)
        grown = 3.0 * (pushed + along(w, i) * pushed) - shared
        values.append(value - (4.0 * LATTICE_WEIGHTS[i]) * grown)
    return values


def interface_rows(pops):
    density = pops[0]
    for i in range(1, 19):
        density = density + pops[i]
    velocity = []
    for k in range(3):
        running = jnp.zeros_like(density)
        for i in range(19):
            if VELOCITIES[i][k] == 1:
                running = running + pops[i]
            elif VELOCITIES[i][k] == -1:
                running = running - pops[i]
        velocity.append(running / density)
    speed_sq = velocity[0] * velocity[0] + velocity[1] * velocity[1] + velocity[2] * velocity[2]
    rows = []
    for i in INWARD:
        dotted = jnp.zeros_like(density)
        for k in range(3):
            if VELOCITIES[i][k] == 1:
                dotted = dotted + velocity[k]
            elif VELOCITIES[i][k] == -1:
                dotted = dotted - velocity[k]
        weight = LATTICE_WEIGHTS[i]
        balance = weight * density * (1.0 + 3.0 * dotted + 4.5 * dotted * dotted - 1.5 * speed_sq)
        rows.append(balance + RESCALE * (pops[i] - balance))
    return rows


def pulled(load, ghost, first_column, low, high):
    lane = lax.broadcasted_iota(jnp.int32, (8, FW), 1)
    inner = lane == 0
    outer = lane == FW - 1
    values = []
    for i in range(19):
        ca, cr, cw = VELOCITIES[i]
        value = load(i, -ca, -cr)
        ended = low if ca == 1 else high if ca == -1 else None
        if cw == 1 or ended is not None:
            reflected = load(opposite(i), 0, 0)
        if cw == 1:
            value = jnp.where(inner, reflected, pltpu.roll(value, 1, 1))
        elif cw == -1:
            shift = FW - 1 - (first_column + INWARD.index(i))
            value = jnp.where(outer, pltpu.roll(ghost, shift, 1), pltpu.roll(value, FW - 1, 1))
        if ended is not None:
            value = jnp.where(ended, reflected, value)
        values.append(value)
    return values


def pull_plane(relaxed, ghosts, first_column, a, half, low, high):
    row = OFF + a * PLANE + half * 8

    def load(i, da, dr):
        return relaxed[SLOT[i], pl.ds(row + da * PLANE + dr, 8), :]

    ghost = ghosts[pl.ds(a * FR + half * 8, 8), :]
    return pulled(load, ghost, first_column, low, high)


def pull_rim(relaxed, margin, ghosts, first_column, c, r, first, last):
    row = OFF + c * (8 * PLANE) + r

    def load(i, da, dr):
        if r + dr < 0:
            return margin[0, FORTH.index(i), pl.ds(8 + c * 8 + da, 8), :]
        if r + dr >= FR:
            return margin[1, BACK.index(i), pl.ds(8 + c * 8 + da, 8), :]
        return relaxed[SLOT[i], pl.ds(row + da * PLANE + dr, 8, stride=PLANE), :]

    ghost = ghosts[pl.ds(c * (8 * FR) + r, 8, stride=FR), :]
    axial = lax.broadcasted_iota(jnp.int32, (8, FW), 0) + c * 8
    low = axial == jnp.where(first, 0, -1)
    high = axial == jnp.where(last, FA - 1, -1)
    return pulled(load, ghost, first_column, low, high)


def end_mask(flag):
    return lax.broadcasted_iota(jnp.int32, (8, FW), 0) < jnp.where(flag, 8, 0)


def split(x):
    high = x.astype(jnp.bfloat16)
    rest = x - high.astype(jnp.float32)
    middle = rest.astype(jnp.bfloat16)
    low = (rest - middle.astype(jnp.float32)).astype(jnp.bfloat16)
    return high, middle, low


def advance(
    n_coarse,
    n_sector,
    fine_hbm,
    face_hbm,
    map_hbm,
    mforce_hbm,
    mweights_hbm,
    tiles_hbm,
    count_ref,
    relaxed2,
    margin2,
    ghosts,
    fine,
    face,
    gmap,
    mforce,
    mweights,
    tiles_ref,
    rows3,
    parts,
    force,
    rims,
    gown,
    gnext,
    relaxed1,
    margin1,
    outbox,
    inbox,
    edges,
    sends,
    local_sem,
    send_sem,
    recv_sem,
):
    p = lax.axis_index("coarse")
    s = lax.axis_index("sector")
    ahead = lax.rem(s + 1, n_sector)
    behind = lax.rem(s + n_sector - 1, n_sector)
    first, last = p == 0, p == n_coarse - 1
    has_low, has_high = p > 0, p < n_coarse - 1

    loads = [
        pltpu.make_async_copy(mweights_hbm, mweights, local_sem.at[0]),
        pltpu.make_async_copy(mforce_hbm, mforce, local_sem.at[1]),
        pltpu.make_async_copy(face_hbm, face, local_sem.at[2]),
        pltpu.make_async_copy(map_hbm, gmap, local_sem.at[3]),
        pltpu.make_async_copy(tiles_hbm, tiles_ref, local_sem.at[8]),
    ]
    for c in range(4):
        rows = pl.ds(c * 128, 128)
        loads.append(
            pltpu.make_async_copy(fine_hbm.at[:, rows, :], fine.at[:, rows, :], local_sem.at[4 + c])
        )
    for copy in loads:
        copy.start()

    barrier = pltpu.get_barrier_semaphore()

    def greet(coarse, sector):
        pl.semaphore_signal(
            barrier, inc=1, device_id={"coarse": coarse, "sector": sector}, device_id_type=MESH
        )

    greet(p, ahead)
    greet(p, behind)
    for there, coarse in ((has_low, p - 1), (has_high, p + 1)):

        @pl.when(there)
        def _():
            greet(coarse, s)
            greet(coarse, ahead)
            greet(coarse, behind)

    loads[1].wait()
    for k in range(3):
        rows3[pl.ds(k, NB, stride=8), :] = mforce[k].astype(jnp.float32)
    loads[0].wait()

    def block(b, carry):
        for k in range(4):
            n = b * 4 + k
            rows = pl.ds(pl.multiple_of(n * 8, 8), 8)
            parts[rows, :] = jnp.dot(
                rows3[rows, :].astype(jnp.bfloat16),
                mweights[n],
                preferred_element_type=jnp.float32,
            )
        return carry

    lax.fori_loop(0, NB // 4, block, 0)
    loads[4].wait()
    block_id = lax.rem(lax.broadcasted_iota(jnp.int32, (8, 3 * NB), 1), NB)
    tile = jnp.zeros((8, 3 * NB), jnp.int32)
    for b in range(NB):
        tile = jnp.where(block_id == b, tiles_ref[b], tile)
    axial = lax.shift_right_logical(tile * 3641, 16)
    cycle = tile - axial * (FR + 2)
    target = jnp.where(
        cycle == 0,
        FA * FR + axial,
        jnp.where(cycle == FR + 1, FA * FR + FA + axial, axial * FR + cycle - 1),
    )
    target = jnp.where(block_id < count_ref[0], target, -1)[:1]
    columns = []
    for k in range(3):
        high, middle, low = split(parts[pl.ds(k, NB, stride=8), :])
        columns.append(jnp.concatenate([high, middle, low], axis=0))
    columns = jnp.concatenate(columns, axis=1)
    for n in range(9):
        cell = lax.broadcasted_iota(jnp.int32, (64, 3 * NB), 0) + n * 64
        chosen = jnp.where(cell == target, 1.0, 0.0).astype(jnp.bfloat16)
        summed = jnp.dot(chosen, columns, preferred_element_type=jnp.float32)
        for k in range(3):
            column = summed[:, k * FW : k * FW + FW]
            if n < 8:
                force[k, n * 64 : n * 64 + 64, :] = column
            else:
                for side in range(2):
                    rim = column[side * FA : side * FA + FA]
                    rims[side, k, 8:40, :] = rim
                    outbox[side, RIM_AT + k, :, :] = rim

    def send(n, src, dst, coarse, sector):
        return pltpu.make_async_remote_copy(
            src_ref=src,
            dst_ref=dst,
            send_sem=send_sem.at[n],
            recv_sem=recv_sem.at[n],
            device_id={"coarse": coarse, "sector": sector},
            device_id_type=MESH,
        )

    loads[2].wait()
    for k in range(2):
        new = 0.5 * (k + 1)
        pops = [
            (1.0 - new) * face[i, 0:1, :] + new * face[i, 1:2, :] for i in range(19)
        ]
        for j, row in enumerate(interface_rows(pops)):
            gown[5 * k + j : 5 * k + j + 1, :] = row * (-4.0, 16.0)[k]
    for j in range(10, 16):
        gown[j : j + 1, :] = jnp.zeros((1, FW), jnp.float32)
    ghost_copy = send(GHOST, gown, gnext, p, behind)
    top, bottom = OFF + (FA - 1) * PLANE, OFF

    def planes(n, relaxed):
        upward = send(
            n,
            relaxed.at[0:5, top : top + FR, :],
            relaxed.at[0:5, bottom - PLANE : bottom - PLANE + FR, :],
            p + 1,
            s,
        )
        downward = send(
            n + 1,
            relaxed.at[5:10, bottom : bottom + FR, :],
            relaxed.at[5:10, top + PLANE : top + PLANE + FR, :],
            p - 1,
            s,
        )
        return upward, downward

    def sides(n, box, there):
        groups = []
        for c in range(CHUNKS):
            at, to = pl.ds(c * 8, 8), pl.ds(8 + c * 8, 8)
            groups.append(
                [
                    send(n + 2 * c, box.at[1, :, at, :], there.at[0, :, to, :], p, ahead),
                    send(n + 2 * c + 1, box.at[0, :, at, :], there.at[1, :, to, :], p, behind),
                ]
            )
        return groups

    def start(group):
        for copy in group:
            copy.start()

    def arrive(group):
        for copy in group:
            copy.wait_recv()

    def leave(group):
        for copy in group:
            copy.wait_send()

    def axially(act, upward, downward, receiving):
        for there, group in (
            (has_low if receiving else has_high, upward),
            (has_high if receiving else has_low, downward),
        ):

            @pl.when(there)
            def _():
                act(group)

    sides1 = sides(FIRST, outbox, inbox)
    n = FIRST + 2 * CHUNKS
    plane_up1, plane_down1 = planes(n, relaxed1)
    small_up, small_down = [], []
    for group, m, coarse, row, there, edge in (
        (small_up, n + 2, p + 1, FA - 1, 7, 0),
        (small_down, n + 6, p - 1, 0, 40, 1),
    ):
        at = pl.ds(row, 1)
        to = pl.ds(there, 1)
        group += [
            send(m, outbox.at[1, 3:PARTS, at, :], inbox.at[0, 3:PARTS, to, :], coarse, ahead),
            send(m + 1, outbox.at[0, 3:PARTS, at, :], inbox.at[1, 3:PARTS, to, :], coarse, behind),
            send(m + 2, outbox.at[:, RIM_AT:PARTS, at, :], rims.at[:, :, to, :], coarse, s),
            send(m + 3, outbox.at[:, V_AT:RIM_AT, at, :], edges.at[edge], coarse, s),
        ]

    sides2 = sides(SECOND, sends, margin2)
    n = SECOND + 2 * CHUNKS
    plane_up2, plane_down2 = planes(n, relaxed2)
    corners_up, corners_down = [], []
    for group, m, coarse, row, there, j in (
        (corners_up, n + 2, p + 1, FA - 1, 7, 4),
        (corners_down, n + 4, p - 1, 0, 40, 3),
    ):
        at = pl.ds(row, 1)
        to = pl.ds(there, 1)
        group += [
            send(m, sends.at[1, j, at, :], margin2.at[0, j, to, :], coarse, ahead),
            send(m + 1, sends.at[0, j, at, :], margin2.at[1, j, to, :], coarse, behind),
        ]

    def keep_plane(relaxed, a, half, values, inside=False):
        rows = pl.ds(pl.multiple_of(OFF + a * PLANE + half * 8, 8), 8)
        for i in range(19):
            if inside:
                row = lax.broadcasted_iota(jnp.int32, (8, FW), 0)
                pltpu.store(relaxed.at[SLOT[i], rows, :], values[i], mask=row != 7 * half)
            else:
                relaxed[SLOT[i], rows, :] = values[i]

    def plane1(a, carry):
        for half in range(2):
            row = pl.multiple_of(a * FR + half * 8, 8)
            f = [fine[i, pl.ds(row, 8), :] for i in range(19)]
            push = [force[k, pl.ds(row, 8), :] for k in range(3)]
            keep_plane(relaxed1, a, half, collide(f, push, 1.0)[0])
        return carry

    def rim0(c):
        for side, r in ((0, 0), (1, FR - 1)):
            rows = pl.ds(c * (8 * FR) + r, 8, stride=FR)
            f = [fine[i, rows, :] for i in range(19)]
            push = [force[k, rows, :] for k in range(3)]
            values, u, inverse = collide(f, push, 1.0)
            cells = slice(c * 8, c * 8 + 8)
            for j, i in enumerate(FORTH if side else BACK):
                outbox[side, j, cells, :] = values[i]
            for k in range(3):
                outbox[side, V_AT + k, cells, :] = 3.0 * u[k] + 0.5625 * inverse * push[k]
            outbox[side, INVERSE_AT, cells, :] = inverse

    for c in range(4):
        loads[5 + c].wait()
        rim0(c)
    plane1(0, 0)
    plane1(FA - 1, 0)

    peers = 2 + jnp.where(has_low, 3, 0) + jnp.where(has_high, 3, 0)
    pl.semaphore_wait(barrier, peers)
    ghost_copy.start()
    axially(start, small_up, small_down, False)
    for group in sides1:
        start(group)
    axially(start, [plane_up1], [plane_down1], False)
    lax.fori_loop(1, FA - 1, plane1, 0, unroll=2)

    loads[3].wait()
    ghost_copy.wait_recv()
    window = jnp.concatenate([gown[...], gnext[...]], axis=1)
    turned = gmap[...]
    cell = lax.broadcasted_iota(jnp.int32, (FR, 2 * FW), 1)
    window_parts = split(window)
    for n in range(4):
        chosen = jnp.concatenate(
            [
                jnp.where(
                    jnp.broadcast_to(turned[:, a : a + 1], (FR, 2 * FW)) == cell, 1.0, 0.0
                )
                for a in range(n * 8, n * 8 + 8)
            ],
            axis=0,
        ).astype(jnp.bfloat16)
        total = jnp.zeros((128, 16), jnp.float32)
        for part in window_parts:
            total = total + lax.dot_general(
                chosen, part, (((1,), (1,)), ((), ())), preferred_element_type=jnp.float32
            )
        ghosts[n * 128 : n * 128 + 128, 0:16] = total

    def plane2(a, low, high):
        for half in range(2):
            f = pull_plane(relaxed1, ghosts, 0, a, half, low, high)
            row = pl.multiple_of(a * FR + half * 8, 8)
            push = [force[k, pl.ds(row, 8), :] for k in range(3)]
            keep_plane(relaxed2, a, half, collide(f, push, -0.25)[0], True)

    def inner2(a, carry):
        plane2(a, None, None)
        return carry

    def keep_rim(relaxed, c, r, values):
        row = OFF + c * (8 * PLANE) + r
        for i in range(19):
            relaxed[SLOT[i], pl.ds(row, 8, stride=PLANE), :] = values[i]

    def rim1(c):
        for side, r in ((0, 0), (1, FR - 1)):
            rows = pl.ds(c * (8 * FR) + r, 8, stride=FR)
            f = [fine[i, rows, :] for i in range(19)]
            cells = slice(8 + c * 8, 16 + c * 8)
            push = [force[k, rows, :] + inbox[side, RIM_AT + k, cells, :] for k in range(3)]
            for k in range(3):
                force[k, rows, :] = push[k]
            keep_rim(relaxed1, c, r, collide(f, push, 1.0)[0])

    def rim2(c):
        for side, r in ((0, 0), (1, FR - 1)):
            f = pull_rim(relaxed1, margin1, ghosts, 0, c, r, first, last)
            rows = pl.ds(c * (8 * FR) + r, 8, stride=FR)
            push = [force[k, rows, :] for k in range(3)]
            values = collide(f, push, -0.25)[0]
            keep_rim(relaxed2, c, r, values)
            for j, i in enumerate(FORTH if side else BACK):
                sends[side, j, c * 8 : c * 8 + 8, :] = values[i]

    def margin_rows(side, cells, which):
        pops = [(BACK if side else FORTH)[j] for j in which]
        values = corrected(
            [inbox[side, j, cells, :] for j in which],
            pops,
            [rims[side, k, cells, :] for k in range(3)],
            [inbox[side, V_AT + k, cells, :] for k in range(3)],
            inbox[side, INVERSE_AT, cells, :],
        )
        for j, value in zip(which, values):
            margin1[side, j, cells, :] = value

    def edge_rows(edge, pops, plane, at):
        for side, r in ((0, 0), (1, FR - 1)):
            row = OFF + plane * PLANE + r
            values = corrected(
                [relaxed1[SLOT[i], row : row + 1, :] for i in pops],
                pops,
                [inbox[side, RIM_AT + k, at : at + 1, :] for k in range(3)],
                [edges[edge, side, k, :, :] for k in range(3)],
                edges[edge, side, 3, :, :],
            )
            for i, value in zip(pops, values):
                relaxed1[SLOT[i], row : row + 1, :] = value

    axially(arrive, [plane_up1], [plane_down1], True)
    axially(leave, [plane_up1], [plane_down1], False)
    axially(arrive, small_up, small_down, True)
    for side in range(2):
        margin_rows(side, slice(7, 8), [4])
        margin_rows(side, slice(40, 41), [3])
    edge_rows(0, UP, -1, 7)
    edge_rows(1, DOWN, FA, 40)
    for c in range(CHUNKS):
        arrive(sides1[c])
        rim1(c)
        for side in range(2):
            margin_rows(side, slice(8 + c * 8, 16 + c * 8), range(5))
        ready = [c - 1] if c > 0 else []
        if c == CHUNKS - 1:
            ready.append(c)
        for done in ready:
            rim2(done)
            start(sides2[done])
            if done == 0:
                axially(start, [], corners_down, False)
    axially(start, corners_up, [], False)
    plane2(0, end_mask(first), None)
    plane2(FA - 1, None, end_mask(last))
    axially(start, [plane_up2], [plane_down2], False)
    lax.fori_loop(1, FA - 1, inner2, 0, unroll=5)
    ghost_copy.wait_send()
    for group in sides1:
        leave(group)
    axially(leave, small_up, small_down, False)
    axially(arrive, [plane_up2] + corners_up, [plane_down2] + corners_down, True)
    for group in sides2:
        arrive(group)
    for group in sides2:
        leave(group)
    axially(leave, [plane_up2] + corners_up, [plane_down2] + corners_down, False)


def settle(n_coarse, relaxed, margin, ghosts, out_hbm, out, sem):
    p = lax.axis_index("coarse")
    first, last = p == 0, p == n_coarse - 1

    def plane(a, low, high):
        for half in range(2):
            f = pull_plane(relaxed, ghosts, 5, a, half, low, high)
            row = pl.multiple_of(a * FR + half * 8, 8)
            for i in range(19):
                out[i, pl.ds(row, 8), :] = f[i] * 0.0625

    def inner(a, carry):
        plane(a, None, None)
        return carry

    copies = []
    for c in range(4):
        if c == 0:
            plane(0, end_mask(first), None)
        lax.fori_loop(max(c * 8, 1), min(c * 8 + 8, FA - 1), inner, 0, unroll=True)
        if c == 3:
            plane(FA - 1, None, end_mask(last))
        for r in (0, FR - 1):
            f = pull_rim(relaxed, margin, ghosts, 5, c, r, first, last)
            for i in range(19):
                out[i, pl.ds(c * (8 * FR) + r, 8, stride=FR), :] = f[i] * 0.0625
        rows = pl.ds(c * 128, 128)
        copy = pltpu.make_async_copy(out.at[:, rows, :], out_hbm.at[:, rows, :], sem.at[c])
        copy.start()
        copies.append(copy)
    for copy in copies:
        copy.wait()


def local(
    fine_populations,
    coarse_face,
    ghost_map,
    marker_force,
    marker_weights,
    marker_tiles,
    block_counts,
):
    n_coarse, n_sector = lax.axis_size("coarse"), lax.axis_size("sector")
    f32 = jnp.float32
    vmem = pl.BlockSpec(memory_space=pltpu.VMEM)
    hbm = pl.BlockSpec(memory_space=pltpu.HBM)
    margin = (2, 5, 48, FW)
    state = pl.pallas_call(
        functools.partial(advance, n_coarse, n_sector),
        out_shape=(
            pltpu.VMEM((19, ROWS, FW), f32),
            pltpu.VMEM(margin, f32),
            pltpu.VMEM((FA * FR, FW), f32),
        ),
        in_specs=[hbm] * 6 + [pl.BlockSpec(memory_space=pltpu.SMEM)],
        out_specs=(vmem, vmem, vmem),
        scratch_shapes=[
            pltpu.VMEM((19, FA * FR, FW), f32),
            pltpu.VMEM((19, 2, FW), f32),
            pltpu.VMEM((FR, FA), jnp.int32),
            pltpu.VMEM((3, NB, MB), jnp.bfloat16),
            pltpu.VMEM((NB, MB, FW), jnp.bfloat16),
            pltpu.SMEM((NB,), jnp.int32),
            pltpu.VMEM((NB * 8, MB), f32),
            pltpu.VMEM((NB * 8, FW), f32),
            pltpu.VMEM((3, FA * FR, FW), f32),
            pltpu.VMEM((2, 3, 48, FW), f32),
            pltpu.VMEM((16, FW), f32),
            pltpu.VMEM((16, FW), f32),
            pltpu.VMEM((19, ROWS, FW), f32),
            pltpu.VMEM(margin, f32),
            pltpu.VMEM((2, PARTS, FA, FW), f32),
            pltpu.VMEM((2, PARTS, 48, FW), f32),
            pltpu.VMEM((2, 2, 4, 1, FW), f32),
            pltpu.VMEM((2, 5, FA, FW), f32),
            pltpu.SemaphoreType.DMA((9,)),
            pltpu.SemaphoreType.DMA((N_REMOTE,)),
            pltpu.SemaphoreType.DMA((N_REMOTE,)),
        ],
        compiler_params=pltpu.CompilerParams(
            collective_id=0, has_side_effects=True, vmem_limit_bytes=32 * 1024 * 1024
        ),
        name="advance",
    )(
        *(
            pltpu.with_memory_space_constraint(x, pltpu.HBM)
            for x in (
                fine_populations.reshape(19, FA * FR, FW),
                jnp.transpose(coarse_face, (1, 0, 2)),
                jnp.transpose(ghost_map),
                jnp.transpose(marker_force, (1, 0, 2)),
                marker_weights,
                marker_tiles,
            )
        ),
        block_counts,
    )
    out = pl.pallas_call(
        functools.partial(settle, n_coarse),
        out_shape=jax.ShapeDtypeStruct((19, FA * FR, FW), f32),
        in_specs=[vmem, vmem, vmem],
        out_specs=hbm,
        scratch_shapes=[
            pltpu.VMEM((19, FA * FR, FW), f32),
            pltpu.SemaphoreType.DMA((4,)),
        ],
        compiler_params=pltpu.CompilerParams(vmem_limit_bytes=32 * 1024 * 1024),
        name="settle",
    )(*state)
    return out.reshape(19, FA, FR, FW)


def solution(mesh):
    in_specs = (
        P(None, "coarse", "sector", None),
        P(None, None, ("coarse", "sector")),
        P("coarse", "sector"),
        P(("coarse", "sector"), None, None),
        P(("coarse", "sector"), None, None),
        P(("coarse", "sector")),
        P(("coarse", "sector")),
    )
    out_specs = P(None, "coarse", "sector", None)
    return jax.shard_map(local, mesh=mesh, in_specs=in_specs, out_specs=out_specs, check_vma=False)
```

```python
import functools

import jax
import jax.numpy as jnp
from jax import lax
from jax.experimental import pallas as pl
from jax.experimental.pallas import tpu as pltpu
from jax.sharding import PartitionSpec as P

VELOCITIES = (
    (0, 0, 0),
    (1, 0, 0),
    (-1, 0, 0),
    (0, 1, 0),
    (0, -1, 0),
    (0, 0, 1),
    (0, 0, -1),
    (1, 1, 0),
    (-1, -1, 0),
    (1, -1, 0),
    (-1, 1, 0),
    (1, 0, 1),
    (-1, 0, -1),
    (1, 0, -1),
    (-1, 0, 1),
    (0, 1, 1),
    (0, -1, -1),
    (0, 1, -1),
    (0, -1, 1),
)
LATTICE_WEIGHTS = (1.0 / 3.0,) + (1.0 / 18.0,) * 6 + (1.0 / 36.0,) * 12
TAU_FINE = 0.8
TAU_COARSE = 0.65
FORCE_FACTOR = 1.0 - 0.5 / TAU_FINE
RESCALE = TAU_FINE / (2.0 * TAU_COARSE)

FA, FR, FW = 32, 16, 128
NB, MB = 32, 128
PLANE = 24
OFF = 32
ROWS = OFF + FA * PLANE + PLANE

UP = [i for i in range(19) if VELOCITIES[i][0] == 1]
DOWN = [i for i in range(19) if VELOCITIES[i][0] == -1]
FORTH = [3, 15, 17, 10, 7]
BACK = [4, 16, 18, 8, 9]
INWARD = [i for i in range(19) if VELOCITIES[i][2] == -1]
ORDER = UP + DOWN + [i for i in range(19) if VELOCITIES[i][0] == 0]
SLOT = {pop: slot for slot, pop in enumerate(ORDER)}

V_AT, INVERSE_AT, RIM_AT, PARTS = 5, 8, 9, 12

GHOST, FIRST, SECOND = 0, 1, 19
N_REMOTE = SECOND + 14
CHUNKS = 4

MESH = pl.DeviceIdType.MESH


def opposite(pop_index):
    if pop_index == 0:
        return 0
    return pop_index + 1 if pop_index % 2 == 1 else pop_index - 1


def collide(f, force, scale):
    gain = -4.0 / scale
    s, d = {}, {}
    for i in range(1, 19, 2):
        s[i] = f[i] + f[i + 1]
        d[i] = f[i] - f[i + 1]
    density = ((f[0] + s[1]) + (s[3] + s[5])) + ((s[7] + s[9]) + (s[11] + s[13])) + (s[15] + s[17])
    momentum = [
        d[1] + (d[7] + d[9]) + (d[11] + d[13]),
        d[3] + (d[7] - d[9]) + (d[15] + d[17]),
        d[5] + (d[11] - d[13]) + (d[15] - d[17]),
    ]
    guess = pl.reciprocal(density, approx=True)
    inverse = guess * (2.0 - density * guess)
    pushed = [momentum[k] + (0.5 / scale) * force[k] for k in range(3)]
    u = [pushed[k] * inverse for k in range(3)]
    h = [(-22.5 / 36.0) * pushed[k] + (gain * 3.375 / 36.0) * force[k] for k in range(3)]
    q = [(-15.0 / 36.0) * pushed[k] + (gain * 1.125 / 36.0) * force[k] for k in range(3)]
    t = [u[k] * h[k] for k in range(3)]
    base = (-5.0 / 36.0) * density - (1.0 / 3.0) * (t[0] + t[1] + t[2])
    out = [None] * 19
    out[0] = f[0] + 12.0 * base
    for k, i in enumerate((1, 3, 5)):
        even = 2.0 * (base + t[k])
        odd = 2.0 * q[k]
        out[i] = f[i] + (even + odd)
        out[i + 1] = f[i + 1] + (even - odd)
    for a, b, i in ((0, 1, 7), (0, 2, 11), (1, 2, 15)):
        common = base + t[a] + t[b]
        cross = u[a] * h[b] + u[b] * h[a]
        for j, even, odd in (
            (i, common + cross, q[a] + q[b]),
            (i + 2, common - cross, q[a] - q[b]),
        ):
            out[j] = f[j] + (even + odd)
            out[j + 1] = f[j + 1] + (even - odd)
    return out, u, inverse


def along(vector, i):
    terms = [vector[k] if VELOCITIES[i][k] == 1 else -vector[k] for k in range(3) if VELOCITIES[i][k]]
    return functools.reduce(lambda x, y: x + y, terms)


def corrected(base, pops, extra, v, inverse):
    w = [v[k] + 1.03125 * inverse * extra[k] for k in range(3)]
    shared = w[0] * extra[0] + w[1] * extra[1] + w[2] * extra[2]
    values = []
    for value, i in zip(base, pops):
        pushed = along(extra, i)
        grown = 3.0 * (pushed + along(w, i) * pushed) - shared
        values.append(value - (4.0 * LATTICE_WEIGHTS[i]) * grown)
    return values


def interface_rows(pops):
    density = pops[0]
    for i in range(1, 19):
        density = density + pops[i]
    velocity = []
    for k in range(3):
        running = jnp.zeros_like(density)
        for i in range(19):
            if VELOCITIES[i][k] == 1:
                running = running + pops[i]
            elif VELOCITIES[i][k] == -1:
                running = running - pops[i]
        velocity.append(running / density)
    speed_sq = velocity[0] * velocity[0] + velocity[1] * velocity[1] + velocity[2] * velocity[2]
    rows = []
    for i in INWARD:
        dotted = jnp.zeros_like(density)
        for k in range(3):
            if VELOCITIES[i][k] == 1:
                dotted = dotted + velocity[k]
            elif VELOCITIES[i][k] == -1:
                dotted = dotted - velocity[k]
        weight = LATTICE_WEIGHTS[i]
        balance = weight * density * (1.0 + 3.0 * dotted + 4.5 * dotted * dotted - 1.5 * speed_sq)
        rows.append(balance + RESCALE * (pops[i] - balance))
    return rows


def pulled(load, ghost, first_column, low, high):
    lane = lax.broadcasted_iota(jnp.int32, (8, FW), 1)
    inner = lane == 0
    outer = lane == FW - 1
    values = []
    for i in range(19):
        ca, cr, cw = VELOCITIES[i]
        value = load(i, -ca, -cr)
        ended = low if ca == 1 else high if ca == -1 else None
        if cw == 1 or ended is not None:
            reflected = load(opposite(i), 0, 0)
        if cw == 1:
            value = jnp.where(inner, reflected, pltpu.roll(value, 1, 1))
        elif cw == -1:
            shift = FW - 1 - (first_column + INWARD.index(i))
            value = jnp.where(outer, pltpu.roll(ghost, shift, 1), pltpu.roll(value, FW - 1, 1))
        if ended is not None:
            value = jnp.where(ended, reflected, value)
        values.append(value)
    return values


def pull_plane(relaxed, ghosts, first_column, a, half, low, high):
    row = OFF + a * PLANE + half * 8

    def load(i, da, dr):
        return relaxed[SLOT[i], pl.ds(row + da * PLANE + dr, 8), :]

    ghost = ghosts[pl.ds(a * FR + half * 8, 8), :]
    return pulled(load, ghost, first_column, low, high)


def pull_rim(relaxed, margin, ghosts, first_column, c, r, first, last):
    row = OFF + c * (8 * PLANE) + r

    def load(i, da, dr):
        if r + dr < 0:
            return margin[0, FORTH.index(i), pl.ds(8 + c * 8 + da, 8), :]
        if r + dr >= FR:
            return margin[1, BACK.index(i), pl.ds(8 + c * 8 + da, 8), :]
        return relaxed[SLOT[i], pl.ds(row + da * PLANE + dr, 8, stride=PLANE), :]

    ghost = ghosts[pl.ds(c * (8 * FR) + r, 8, stride=FR), :]
    axial = lax.broadcasted_iota(jnp.int32, (8, FW), 0) + c * 8
    low = axial == jnp.where(first, 0, -1)
    high = axial == jnp.where(last, FA - 1, -1)
    return pulled(load, ghost, first_column, low, high)


def end_mask(flag):
    return lax.broadcasted_iota(jnp.int32, (8, FW), 0) < jnp.where(flag, 8, 0)


def split(x):
    high = x.astype(jnp.bfloat16)
    rest = x - high.astype(jnp.float32)
    middle = rest.astype(jnp.bfloat16)
    low = (rest - middle.astype(jnp.float32)).astype(jnp.bfloat16)
    return high, middle, low


def advance(
    n_coarse,
    n_sector,
    fine_hbm,
    face_hbm,
    map_hbm,
    mforce_hbm,
    mweights_hbm,
    tiles_hbm,
    count_ref,
    relaxed2,
    margin2,
    ghosts,
    fine,
    face,
    gmap,
    mforce,
    mweights,
    tiles_ref,
    rows3,
    parts,
    force,
    rims,
    gown,
    gnext,
    relaxed1,
    margin1,
    outbox,
    inbox,
    edges,
    sends,
    local_sem,
    send_sem,
    recv_sem,
):
    p = lax.axis_index("coarse")
    s = lax.axis_index("sector")
    ahead = lax.rem(s + 1, n_sector)
    behind = lax.rem(s + n_sector - 1, n_sector)
    first, last = p == 0, p == n_coarse - 1
    has_low, has_high = p > 0, p < n_coarse - 1

    loads = [
        pltpu.make_async_copy(mweights_hbm, mweights, local_sem.at[0]),
        pltpu.make_async_copy(mforce_hbm, mforce, local_sem.at[1]),
        pltpu.make_async_copy(face_hbm, face, local_sem.at[2]),
        pltpu.make_async_copy(map_hbm, gmap, local_sem.at[3]),
        pltpu.make_async_copy(tiles_hbm, tiles_ref, local_sem.at[8]),
    ]
    for c in range(4):
        rows = pl.ds(c * 128, 128)
        loads.append(
            pltpu.make_async_copy(fine_hbm.at[:, rows, :], fine.at[:, rows, :], local_sem.at[4 + c])
        )
    for copy in loads:
        copy.start()

    barrier = pltpu.get_barrier_semaphore()

    def greet(coarse, sector):
        pl.semaphore_signal(
            barrier, inc=1, device_id={"coarse": coarse, "sector": sector}, device_id_type=MESH
        )

    greet(p, ahead)
    greet(p, behind)
    for there, coarse in ((has_low, p - 1), (has_high, p + 1)):

        @pl.when(there)
        def _():
            greet(coarse, s)
            greet(coarse, ahead)
            greet(coarse, behind)

    loads[1].wait()
    for k in range(3):
        rows3[pl.ds(k, NB, stride=8), :] = mforce[k].astype(jnp.float32)
    loads[0].wait()

    def block(b, carry):
        for k in range(4):
            n = b * 4 + k
            rows = pl.ds(pl.multiple_of(n * 8, 8), 8)
            parts[rows, :] = jnp.dot(
                rows3[rows, :].astype(jnp.bfloat16),
                mweights[n],
                preferred_element_type=jnp.float32,
            )
        return carry

    lax.fori_loop(0, NB // 4, block, 0)
    loads[4].wait()
    block_id = lax.rem(lax.broadcasted_iota(jnp.int32, (8, 3 * NB), 1), NB)
    tile = jnp.zeros((8, 3 * NB), jnp.int32)
    for b in range(NB):
        tile = jnp.where(block_id == b, tiles_ref[b], tile)
    axial = lax.shift_right_logical(tile * 3641, 16)
    cycle = tile - axial * (FR + 2)
    target = jnp.where(
        cycle == 0,
        FA * FR + axial,
        jnp.where(cycle == FR + 1, FA * FR + FA + axial, axial * FR + cycle - 1),
    )
    target = jnp.where(block_id < count_ref[0], target, -1)[:1]
    columns = []
    for k in range(3):
        high, middle, low = split(parts[pl.ds(k, NB, stride=8), :])
        columns.append(jnp.concatenate([high, middle, low], axis=0))
    columns = jnp.concatenate(columns, axis=1)
    for n in range(9):
        cell = lax.broadcasted_iota(jnp.int32, (64, 3 * NB), 0) + n * 64
        chosen = jnp.where(cell == target, 1.0, 0.0).astype(jnp.bfloat16)
        summed = jnp.dot(chosen, columns, preferred_element_type=jnp.float32)
        for k in range(3):
            column = summed[:, k * FW : k * FW + FW]
            if n < 8:
                force[k, n * 64 : n * 64 + 64, :] = column
            else:
                for side in range(2):
                    rim = column[side * FA : side * FA + FA]
                    rims[side, k, 8:40, :] = rim
                    outbox[side, RIM_AT + k, :, :] = rim

    def send(n, src, dst, coarse, sector):
        return pltpu.make_async_remote_copy(
            src_ref=src,
            dst_ref=dst,
            send_sem=send_sem.at[n],
            recv_sem=recv_sem.at[n],
            device_id={"coarse": coarse, "sector": sector},
            device_id_type=MESH,
        )

    loads[2].wait()
    for k in range(2):
        new = 0.5 * (k + 1)
        pops = [
            (1.0 - new) * face[i, 0:1, :] + new * face[i, 1:2, :] for i in range(19)
        ]
        for j, row in enumerate(interface_rows(pops)):
            gown[5 * k + j : 5 * k + j + 1, :] = row * (-4.0, 16.0)[k]
    for j in range(10, 16):
        gown[j : j + 1, :] = jnp.zeros((1, FW), jnp.float32)
    ghost_copy = send(GHOST, gown, gnext, p, behind)
    top, bottom = OFF + (FA - 1) * PLANE, OFF

    def planes(n, relaxed):
        upward = send(
            n,
            relaxed.at[0:5, top : top + FR, :],
            relaxed.at[0:5, bottom - PLANE : bottom - PLANE + FR, :],
            p + 1,
            s,
        )
        downward = send(
            n + 1,
            relaxed.at[5:10, bottom : bottom + FR, :],
            relaxed.at[5:10, top + PLANE : top + PLANE + FR, :],
            p - 1,
            s,
        )
        return upward, downward

    def sides(n, box, there):
        groups = []
        for c in range(CHUNKS):
            at, to = pl.ds(c * 8, 8), pl.ds(8 + c * 8, 8)
            groups.append(
                [
                    send(n + 2 * c, box.at[1, :, at, :], there.at[0, :, to, :], p, ahead),
                    send(n + 2 * c + 1, box.at[0, :, at, :], there.at[1, :, to, :], p, behind),
                ]
            )
        return groups

    def start(group):
        for copy in group:
            copy.start()

    def arrive(group):
        for copy in group:
            copy.wait_recv()

    def leave(group):
        for copy in group:
            copy.wait_send()

    def axially(act, upward, downward, receiving):
        for there, group in (
            (has_low if receiving else has_high, upward),
            (has_high if receiving else has_low, downward),
        ):

            @pl.when(there)
            def _():
                act(group)

    sides1 = sides(FIRST, outbox, inbox)
    n = FIRST + 2 * CHUNKS
    plane_up1, plane_down1 = planes(n, relaxed1)
    small_up, small_down = [], []
    for group, m, coarse, row, there, edge in (
        (small_up, n + 2, p + 1, FA - 1, 7, 0),
        (small_down, n + 6, p - 1, 0, 40, 1),
    ):
        at = pl.ds(row, 1)
        to = pl.ds(there, 1)
        group += [
            send(m, outbox.at[1, 3:PARTS, at, :], inbox.at[0, 3:PARTS, to, :], coarse, ahead),
            send(m + 1, outbox.at[0, 3:PARTS, at, :], inbox.at[1, 3:PARTS, to, :], coarse, behind),
            send(m + 2, outbox.at[:, RIM_AT:PARTS, at, :], rims.at[:, :, to, :], coarse, s),
            send(m + 3, outbox.at[:, V_AT:RIM_AT, at, :], edges.at[edge], coarse, s),
        ]

    sides2 = sides(SECOND, sends, margin2)
    n = SECOND + 2 * CHUNKS
    plane_up2, plane_down2 = planes(n, relaxed2)
    corners_up, corners_down = [], []
    for group, m, coarse, row, there, j in (
        (corners_up, n + 2, p + 1, FA - 1, 7, 4),
        (corners_down, n + 4, p - 1, 0, 40, 3),
    ):
        at = pl.ds(row, 1)
        to = pl.ds(there, 1)
        group += [
            send(m, sends.at[1, j, at, :], margin2.at[0, j, to, :], coarse, ahead),
            send(m + 1, sends.at[0, j, at, :], margin2.at[1, j, to, :], coarse, behind),
        ]

    def keep_plane(relaxed, a, half, values, inside=False):
        rows = pl.ds(pl.multiple_of(OFF + a * PLANE + half * 8, 8), 8)
        for i in range(19):
            if inside:
                row = lax.broadcasted_iota(jnp.int32, (8, FW), 0)
                pltpu.store(relaxed.at[SLOT[i], rows, :], values[i], mask=row != 7 * half)
            else:
                relaxed[SLOT[i], rows, :] = values[i]

    def plane1(a, carry):
        for half in range(2):
            row = pl.multiple_of(a * FR + half * 8, 8)
            f = [fine[i, pl.ds(row, 8), :] for i in range(19)]
            push = [force[k, pl.ds(row, 8), :] for k in range(3)]
            keep_plane(relaxed1, a, half, collide(f, push, 1.0)[0])
        return carry

    def rim0(c):
        for side, r in ((0, 0), (1, FR - 1)):
            rows = pl.ds(c * (8 * FR) + r, 8, stride=FR)
            f = [fine[i, rows, :] for i in range(19)]
            push = [force[k, rows, :] for k in range(3)]
            values, u, inverse = collide(f, push, 1.0)
            cells = slice(c * 8, c * 8 + 8)
            for j, i in enumerate(FORTH if side else BACK):
                outbox[side, j, cells, :] = values[i]
            for k in range(3):
                outbox[side, V_AT + k, cells, :] = 3.0 * u[k] + 0.5625 * inverse * push[k]
            outbox[side, INVERSE_AT, cells, :] = inverse

    for c in range(4):
        loads[5 + c].wait()
        rim0(c)
    plane1(0, 0)
    plane1(FA - 1, 0)

    peers = 2 + jnp.where(has_low, 3, 0) + jnp.where(has_high, 3, 0)
    pl.semaphore_wait(barrier, peers)
    ghost_copy.start()
    axially(start, small_up, small_down, False)
    for group in sides1:
        start(group)
    axially(start, [plane_up1], [plane_down1], False)
    lax.fori_loop(1, FA - 1, plane1, 0, unroll=2)

    loads[3].wait()
    ghost_copy.wait_recv()
    window = jnp.concatenate([gown[...], gnext[...]], axis=1)
    turned = gmap[...]
    cell = lax.broadcasted_iota(jnp.int32, (FR, 2 * FW), 1)
    window_parts = split(window)
    for n in range(4):
        chosen = jnp.concatenate(
            [
                jnp.where(
                    jnp.broadcast_to(turned[:, a : a + 1], (FR, 2 * FW)) == cell, 1.0, 0.0
                )
                for a in range(n * 8, n * 8 + 8)
            ],
            axis=0,
        ).astype(jnp.bfloat16)
        total = jnp.zeros((128, 16), jnp.float32)
        for part in window_parts:
            total = total + lax.dot_general(
                chosen, part, (((1,), (1,)), ((), ())), preferred_element_type=jnp.float32
            )
        ghosts[n * 128 : n * 128 + 128, 0:16] = total

    def plane2(a, low, high):
        for half in range(2):
            f = pull_plane(relaxed1, ghosts, 0, a, half, low, high)
            row = pl.multiple_of(a * FR + half * 8, 8)
            push = [force[k, pl.ds(row, 8), :] for k in range(3)]
            keep_plane(relaxed2, a, half, collide(f, push, -0.25)[0], True)

    def inner2(a, carry):
        plane2(a, None, None)
        return carry

    def keep_rim(relaxed, c, r, values):
        row = OFF + c * (8 * PLANE) + r
        for i in range(19):
            relaxed[SLOT[i], pl.ds(row, 8, stride=PLANE), :] = values[i]

    def rim1(c):
        for side, r in ((0, 0), (1, FR - 1)):
            rows = pl.ds(c * (8 * FR) + r, 8, stride=FR)
            f = [fine[i, rows, :] for i in range(19)]
            cells = slice(8 + c * 8, 16 + c * 8)
            push = [force[k, rows, :] + inbox[side, RIM_AT + k, cells, :] for k in range(3)]
            for k in range(3):
                force[k, rows, :] = push[k]
            keep_rim(relaxed1, c, r, collide(f, push, 1.0)[0])

    def rim2(c):
        for side, r in ((0, 0), (1, FR - 1)):
            f = pull_rim(relaxed1, margin1, ghosts, 0, c, r, first, last)
            rows = pl.ds(c * (8 * FR) + r, 8, stride=FR)
            push = [force[k, rows, :] for k in range(3)]
            values = collide(f, push, -0.25)[0]
            keep_rim(relaxed2, c, r, values)
            for j, i in enumerate(FORTH if side else BACK):
                sends[side, j, c * 8 : c * 8 + 8, :] = values[i]

    def margin_rows(side, cells, which):
        pops = [(BACK if side else FORTH)[j] for j in which]
        values = corrected(
            [inbox[side, j, cells, :] for j in which],
            pops,
            [rims[side, k, cells, :] for k in range(3)],
            [inbox[side, V_AT + k, cells, :] for k in range(3)],
            inbox[side, INVERSE_AT, cells, :],
        )
        for j, value in zip(which, values):
            margin1[side, j, cells, :] = value

    def edge_rows(edge, pops, plane, at):
        for side, r in ((0, 0), (1, FR - 1)):
            row = OFF + plane * PLANE + r
            values = corrected(
                [relaxed1[SLOT[i], row : row + 1, :] for i in pops],
                pops,
                [inbox[side, RIM_AT + k, at : at + 1, :] for k in range(3)],
                [edges[edge, side, k, :, :] for k in range(3)],
                edges[edge, side, 3, :, :],
            )
            for i, value in zip(pops, values):
                relaxed1[SLOT[i], row : row + 1, :] = value

    axially(arrive, [plane_up1], [plane_down1], True)
    axially(leave, [plane_up1], [plane_down1], False)
    axially(arrive, small_up, small_down, True)
    for side in range(2):
        margin_rows(side, slice(7, 8), [4])
        margin_rows(side, slice(40, 41), [3])
    edge_rows(0, UP, -1, 7)
    edge_rows(1, DOWN, FA, 40)
    for c in range(CHUNKS):
        arrive(sides1[c])
        rim1(c)
        for side in range(2):
            margin_rows(side, slice(8 + c * 8, 16 + c * 8), range(5))
        ready = [c - 1] if c > 0 else []
        if c == CHUNKS - 1:
            ready.append(c)
        for done in ready[::-1]:
            rim2(done)
            if done == 0:
                axially(start, [], corners_down, False)
            if done == CHUNKS - 1:
                axially(start, corners_up, [], False)
            start(sides2[done])
    plane2(0, end_mask(first), None)
    plane2(FA - 1, None, end_mask(last))
    axially(start, [plane_up2], [plane_down2], False)
    lax.fori_loop(1, FA - 1, inner2, 0, unroll=5)
    ghost_copy.wait_send()
    for group in sides1:
        leave(group)
    axially(leave, small_up, small_down, False)
    axially(arrive, [plane_up2] + corners_up, [plane_down2] + corners_down, True)
    for group in sides2:
        arrive(group)
    for group in sides2:
        leave(group)
    axially(leave, [plane_up2] + corners_up, [plane_down2] + corners_down, False)


def settle(n_coarse, relaxed, margin, ghosts, out_hbm, out, sem):
    p = lax.axis_index("coarse")
    first, last = p == 0, p == n_coarse - 1

    def plane(a, low, high):
        for half in range(2):
            f = pull_plane(relaxed, ghosts, 5, a, half, low, high)
            row = pl.multiple_of(a * FR + half * 8, 8)
            for i in range(19):
                out[i, pl.ds(row, 8), :] = f[i] * 0.0625

    def inner(a, carry):
        plane(a, None, None)
        return carry

    copies = []
    for c in range(4):
        if c == 0:
            plane(0, end_mask(first), None)
        lax.fori_loop(max(c * 8, 1), min(c * 8 + 8, FA - 1), inner, 0, unroll=True)
        if c == 3:
            plane(FA - 1, None, end_mask(last))
        for r in (0, FR - 1):
            f = pull_rim(relaxed, margin, ghosts, 5, c, r, first, last)
            for i in range(19):
                out[i, pl.ds(c * (8 * FR) + r, 8, stride=FR), :] = f[i] * 0.0625
        rows = pl.ds(c * 128, 128)
        copy = pltpu.make_async_copy(out.at[:, rows, :], out_hbm.at[:, rows, :], sem.at[c])
        copy.start()
        copies.append(copy)
    for copy in copies:
        copy.wait()


def local(
    fine_populations,
    coarse_face,
    ghost_map,
    marker_force,
    marker_weights,
    marker_tiles,
    block_counts,
):
    n_coarse, n_sector = lax.axis_size("coarse"), lax.axis_size("sector")
    f32 = jnp.float32
    vmem = pl.BlockSpec(memory_space=pltpu.VMEM)
    hbm = pl.BlockSpec(memory_space=pltpu.HBM)
    margin = (2, 5, 48, FW)
    state = pl.pallas_call(
        functools.partial(advance, n_coarse, n_sector),
        out_shape=(
            pltpu.VMEM((19, ROWS, FW), f32),
            pltpu.VMEM(margin, f32),
            pltpu.VMEM((FA * FR, FW), f32),
        ),
        in_specs=[hbm] * 6 + [pl.BlockSpec(memory_space=pltpu.SMEM)],
        out_specs=(vmem, vmem, vmem),
        scratch_shapes=[
            pltpu.VMEM((19, FA * FR, FW), f32),
            pltpu.VMEM((19, 2, FW), f32),
            pltpu.VMEM((FR, FA), jnp.int32),
            pltpu.VMEM((3, NB, MB), jnp.bfloat16),
            pltpu.VMEM((NB, MB, FW), jnp.bfloat16),
            pltpu.SMEM((NB,), jnp.int32),
            pltpu.VMEM((NB * 8, MB), f32),
            pltpu.VMEM((NB * 8, FW), f32),
            pltpu.VMEM((3, FA * FR, FW), f32),
            pltpu.VMEM((2, 3, 48, FW), f32),
            pltpu.VMEM((16, FW), f32),
            pltpu.VMEM((16, FW), f32),
            pltpu.VMEM((19, ROWS, FW), f32),
            pltpu.VMEM(margin, f32),
            pltpu.VMEM((2, PARTS, FA, FW), f32),
            pltpu.VMEM((2, PARTS, 48, FW), f32),
            pltpu.VMEM((2, 2, 4, 1, FW), f32),
            pltpu.VMEM((2, 5, FA, FW), f32),
            pltpu.SemaphoreType.DMA((9,)),
            pltpu.SemaphoreType.DMA((N_REMOTE,)),
            pltpu.SemaphoreType.DMA((N_REMOTE,)),
        ],
        compiler_params=pltpu.CompilerParams(
            collective_id=0, has_side_effects=True, vmem_limit_bytes=32 * 1024 * 1024
        ),
        name="advance",
    )(
        *(
            pltpu.with_memory_space_constraint(x, pltpu.HBM)
            for x in (
                fine_populations.reshape(19, FA * FR, FW),
                jnp.transpose(coarse_face, (1, 0, 2)),
                jnp.transpose(ghost_map),
                jnp.transpose(marker_force, (1, 0, 2)),
                marker_weights,
                marker_tiles,
            )
        ),
        block_counts,
    )
    out = pl.pallas_call(
        functools.partial(settle, n_coarse),
        out_shape=jax.ShapeDtypeStruct((19, FA * FR, FW), f32),
        in_specs=[vmem, vmem, vmem],
        out_specs=hbm,
        scratch_shapes=[
            pltpu.VMEM((19, FA * FR, FW), f32),
            pltpu.SemaphoreType.DMA((4,)),
        ],
        compiler_params=pltpu.CompilerParams(vmem_limit_bytes=32 * 1024 * 1024),
        name="settle",
    )(*state)
    return out.reshape(19, FA, FR, FW)


def solution(mesh):
    in_specs = (
        P(None, "coarse", "sector", None),
        P(None, None, ("coarse", "sector")),
        P("coarse", "sector"),
        P(("coarse", "sector"), None, None),
        P(("coarse", "sector"), None, None),
        P(("coarse", "sector")),
        P(("coarse", "sector")),
    )
    out_specs = P(None, "coarse", "sector", None)
    return jax.shard_map(local, mesh=mesh, in_specs=in_specs, out_specs=out_specs, check_vma=False)
```

```python
import functools

import jax
import jax.numpy as jnp
from jax import lax
from jax.experimental import pallas as pl
from jax.experimental.pallas import tpu as pltpu
from jax.sharding import PartitionSpec as P

VELOCITIES = (
    (0, 0, 0),
    (1, 0, 0),
    (-1, 0, 0),
    (0, 1, 0),
    (0, -1, 0),
    (0, 0, 1),
    (0, 0, -1),
    (1, 1, 0),
    (-1, -1, 0),
    (1, -1, 0),
    (-1, 1, 0),
    (1, 0, 1),
    (-1, 0, -1),
    (1, 0, -1),
    (-1, 0, 1),
    (0, 1, 1),
    (0, -1, -1),
    (0, 1, -1),
    (0, -1, 1),
)
LATTICE_WEIGHTS = (1.0 / 3.0,) + (1.0 / 18.0,) * 6 + (1.0 / 36.0,) * 12
TAU_FINE = 0.8
TAU_COARSE = 0.65
FORCE_FACTOR = 1.0 - 0.5 / TAU_FINE
RESCALE = TAU_FINE / (2.0 * TAU_COARSE)

FA, FR, FW = 32, 16, 128
NB, MB = 32, 128
PLANE = 24
OFF = 32
ROWS = OFF + FA * PLANE + PLANE

UP = [i for i in range(19) if VELOCITIES[i][0] == 1]
DOWN = [i for i in range(19) if VELOCITIES[i][0] == -1]
FORTH = [3, 15, 17, 10, 7]
BACK = [4, 16, 18, 8, 9]
INWARD = [i for i in range(19) if VELOCITIES[i][2] == -1]
ORDER = UP + DOWN + [i for i in range(19) if VELOCITIES[i][0] == 0]
SLOT = {pop: slot for slot, pop in enumerate(ORDER)}

V_AT, INVERSE_AT, RIM_AT, PARTS = 5, 8, 9, 12

GHOST, FIRST, SECOND = 0, 1, 19
N_REMOTE = SECOND + 14
CHUNKS = 4
FIRST_ROWS = ((0, 9), (9, 8), (17, 6), (23, 9))
FIRST_STARTS = ((0, 1), (9,), (16,), (23, 24))
ALIGNED_ROWS = ((0, 8), (8, 8), (16, 8), (24, 8))

MESH = pl.DeviceIdType.MESH


def opposite(pop_index):
    if pop_index == 0:
        return 0
    return pop_index + 1 if pop_index % 2 == 1 else pop_index - 1


def collide(f, force, scale):
    gain = -4.0 / scale
    s, d = {}, {}
    for i in range(1, 19, 2):
        s[i] = f[i] + f[i + 1]
        d[i] = f[i] - f[i + 1]
    density = ((f[0] + s[1]) + (s[3] + s[5])) + ((s[7] + s[9]) + (s[11] + s[13])) + (s[15] + s[17])
    momentum = [
        d[1] + (d[7] + d[9]) + (d[11] + d[13]),
        d[3] + (d[7] - d[9]) + (d[15] + d[17]),
        d[5] + (d[11] - d[13]) + (d[15] - d[17]),
    ]
    guess = pl.reciprocal(density, approx=True)
    inverse = guess * (2.0 - density * guess)
    pushed = [momentum[k] + (0.5 / scale) * force[k] for k in range(3)]
    u = [pushed[k] * inverse for k in range(3)]
    h = [(-22.5 / 36.0) * pushed[k] + (gain * 3.375 / 36.0) * force[k] for k in range(3)]
    q = [(-15.0 / 36.0) * pushed[k] + (gain * 1.125 / 36.0) * force[k] for k in range(3)]
    t = [u[k] * h[k] for k in range(3)]
    base = (-5.0 / 36.0) * density - (1.0 / 3.0) * (t[0] + t[1] + t[2])
    out = [None] * 19
    out[0] = f[0] + 12.0 * base
    for k, i in enumerate((1, 3, 5)):
        even = 2.0 * (base + t[k])
        odd = 2.0 * q[k]
        out[i] = f[i] + (even + odd)
        out[i + 1] = f[i + 1] + (even - odd)
    for a, b, i in ((0, 1, 7), (0, 2, 11), (1, 2, 15)):
        common = base + t[a] + t[b]
        cross = u[a] * h[b] + u[b] * h[a]
        for j, even, odd in (
            (i, common + cross, q[a] + q[b]),
            (i + 2, common - cross, q[a] - q[b]),
        ):
            out[j] = f[j] + (even + odd)
            out[j + 1] = f[j + 1] + (even - odd)
    return out, u, inverse


def along(vector, i):
    terms = [vector[k] if VELOCITIES[i][k] == 1 else -vector[k] for k in range(3) if VELOCITIES[i][k]]
    return functools.reduce(lambda x, y: x + y, terms)


def corrected(base, pops, extra, v, inverse):
    w = [v[k] + 1.03125 * inverse * extra[k] for k in range(3)]
    shared = w[0] * extra[0] + w[1] * extra[1] + w[2] * extra[2]
    values = []
    for value, i in zip(base, pops):
        pushed = along(extra, i)
        grown = 3.0 * (pushed + along(w, i) * pushed) - shared
        values.append(value - (4.0 * LATTICE_WEIGHTS[i]) * grown)
    return values


def interface_rows(pops):
    density = pops[0]
    for i in range(1, 19):
        density = density + pops[i]
    velocity = []
    for k in range(3):
        running = jnp.zeros_like(density)
        for i in range(19):
            if VELOCITIES[i][k] == 1:
                running = running + pops[i]
            elif VELOCITIES[i][k] == -1:
                running = running - pops[i]
        velocity.append(running / density)
    speed_sq = velocity[0] * velocity[0] + velocity[1] * velocity[1] + velocity[2] * velocity[2]
    rows = []
    for i in INWARD:
        dotted = jnp.zeros_like(density)
        for k in range(3):
            if VELOCITIES[i][k] == 1:
                dotted = dotted + velocity[k]
            elif VELOCITIES[i][k] == -1:
                dotted = dotted - velocity[k]
        weight = LATTICE_WEIGHTS[i]
        balance = weight * density * (1.0 + 3.0 * dotted + 4.5 * dotted * dotted - 1.5 * speed_sq)
        rows.append(balance + RESCALE * (pops[i] - balance))
    return rows


def pulled(load, ghost, first_column, low, high):
    lane = lax.broadcasted_iota(jnp.int32, (8, FW), 1)
    inner = lane == 0
    outer = lane == FW - 1
    values = []
    for i in range(19):
        ca, cr, cw = VELOCITIES[i]
        value = load(i, -ca, -cr)
        ended = low if ca == 1 else high if ca == -1 else None
        if cw == 1 or ended is not None:
            reflected = load(opposite(i), 0, 0)
        if cw == 1:
            value = jnp.where(inner, reflected, pltpu.roll(value, 1, 1))
        elif cw == -1:
            shift = FW - 1 - (first_column + INWARD.index(i))
            value = jnp.where(outer, pltpu.roll(ghost, shift, 1), pltpu.roll(value, FW - 1, 1))
        if ended is not None:
            value = jnp.where(ended, reflected, value)
        values.append(value)
    return values


def pull_plane(relaxed, ghosts, first_column, a, half, low, high):
    row = OFF + a * PLANE + half * 8

    def load(i, da, dr):
        return relaxed[SLOT[i], pl.ds(row + da * PLANE + dr, 8), :]

    ghost = ghosts[pl.ds(a * FR + half * 8, 8), :]
    return pulled(load, ghost, first_column, low, high)


def pull_rim(relaxed, margin, ghosts, first_column, c, r, first, last):
    row = OFF + c * (8 * PLANE) + r

    def load(i, da, dr):
        if r + dr < 0:
            return margin[0, FORTH.index(i), pl.ds(8 + c * 8 + da, 8), :]
        if r + dr >= FR:
            return margin[1, BACK.index(i), pl.ds(8 + c * 8 + da, 8), :]
        return relaxed[SLOT[i], pl.ds(row + da * PLANE + dr, 8, stride=PLANE), :]

    ghost = ghosts[pl.ds(c * (8 * FR) + r, 8, stride=FR), :]
    axial = lax.broadcasted_iota(jnp.int32, (8, FW), 0) + c * 8
    low = axial == jnp.where(first, 0, -1)
    high = axial == jnp.where(last, FA - 1, -1)
    return pulled(load, ghost, first_column, low, high)


def end_mask(flag):
    return lax.broadcasted_iota(jnp.int32, (8, FW), 0) < jnp.where(flag, 8, 0)


def split(x):
    high = x.astype(jnp.bfloat16)
    rest = x - high.astype(jnp.float32)
    middle = rest.astype(jnp.bfloat16)
    low = (rest - middle.astype(jnp.float32)).astype(jnp.bfloat16)
    return high, middle, low


def advance(
    n_coarse,
    n_sector,
    fine_hbm,
    face_hbm,
    map_hbm,
    mforce_hbm,
    mweights_hbm,
    tiles_hbm,
    count_ref,
    relaxed2,
    margin2,
    ghosts,
    fine,
    face,
    gmap,
    mforce,
    mweights,
    tiles_ref,
    rows3,
    parts,
    force,
    rims,
    gown,
    gnext,
    relaxed1,
    margin1,
    outbox,
    inbox,
    edges,
    sends,
    local_sem,
    send_sem,
    recv_sem,
):
    p = lax.axis_index("coarse")
    s = lax.axis_index("sector")
    ahead = lax.rem(s + 1, n_sector)
    behind = lax.rem(s + n_sector - 1, n_sector)
    first, last = p == 0, p == n_coarse - 1
    has_low, has_high = p > 0, p < n_coarse - 1

    loads = [
        pltpu.make_async_copy(mweights_hbm, mweights, local_sem.at[0]),
        pltpu.make_async_copy(mforce_hbm, mforce, local_sem.at[1]),
        pltpu.make_async_copy(face_hbm, face, local_sem.at[2]),
        pltpu.make_async_copy(map_hbm, gmap, local_sem.at[3]),
        pltpu.make_async_copy(tiles_hbm, tiles_ref, local_sem.at[8]),
    ]
    for c in range(4):
        rows = pl.ds(c * 128, 128)
        loads.append(
            pltpu.make_async_copy(fine_hbm.at[:, rows, :], fine.at[:, rows, :], local_sem.at[4 + c])
        )
    for copy in loads:
        copy.start()

    barrier = pltpu.get_barrier_semaphore()

    def greet(coarse, sector):
        pl.semaphore_signal(
            barrier, inc=1, device_id={"coarse": coarse, "sector": sector}, device_id_type=MESH
        )

    greet(p, ahead)
    greet(p, behind)
    for there, coarse in ((has_low, p - 1), (has_high, p + 1)):

        @pl.when(there)
        def _():
            greet(coarse, s)
            greet(coarse, ahead)
            greet(coarse, behind)

    loads[1].wait()
    for k in range(3):
        rows3[pl.ds(k, NB, stride=8), :] = mforce[k].astype(jnp.float32)
    loads[0].wait()

    def block(b, carry):
        for k in range(4):
            n = b * 4 + k
            rows = pl.ds(pl.multiple_of(n * 8, 8), 8)
            parts[rows, :] = jnp.dot(
                rows3[rows, :].astype(jnp.bfloat16),
                mweights[n],
                preferred_element_type=jnp.float32,
            )
        return carry

    lax.fori_loop(0, NB // 4, block, 0)
    loads[4].wait()
    block_id = lax.rem(lax.broadcasted_iota(jnp.int32, (8, 3 * NB), 1), NB)
    tile = jnp.zeros((8, 3 * NB), jnp.int32)
    for b in range(NB):
        tile = jnp.where(block_id == b, tiles_ref[b], tile)
    axial = lax.shift_right_logical(tile * 3641, 16)
    cycle = tile - axial * (FR + 2)
    target = jnp.where(
        cycle == 0,
        FA * FR + axial,
        jnp.where(cycle == FR + 1, FA * FR + FA + axial, axial * FR + cycle - 1),
    )
    target = jnp.where(block_id < count_ref[0], target, -1)[:1]
    columns = []
    for k in range(3):
        high, middle, low = split(parts[pl.ds(k, NB, stride=8), :])
        columns.append(jnp.concatenate([high, middle, low], axis=0))
    columns = jnp.concatenate(columns, axis=1)
    for n in range(9):
        cell = lax.broadcasted_iota(jnp.int32, (64, 3 * NB), 0) + n * 64
        chosen = jnp.where(cell == target, 1.0, 0.0).astype(jnp.bfloat16)
        summed = jnp.dot(chosen, columns, preferred_element_type=jnp.float32)
        for k in range(3):
            column = summed[:, k * FW : k * FW + FW]
            if n < 8:
                force[k, n * 64 : n * 64 + 64, :] = column
            else:
                for side in range(2):
                    rim = column[side * FA : side * FA + FA]
                    rims[side, k, 8:40, :] = rim
                    outbox[side, RIM_AT + k, :, :] = rim

    def send(n, src, dst, coarse, sector):
        return pltpu.make_async_remote_copy(
            src_ref=src,
            dst_ref=dst,
            send_sem=send_sem.at[n],
            recv_sem=recv_sem.at[n],
            device_id={"coarse": coarse, "sector": sector},
            device_id_type=MESH,
        )

    loads[2].wait()
    for k in range(2):
        new = 0.5 * (k + 1)
        pops = [
            (1.0 - new) * face[i, 0:1, :] + new * face[i, 1:2, :] for i in range(19)
        ]
        for j, row in enumerate(interface_rows(pops)):
            gown[5 * k + j : 5 * k + j + 1, :] = row * (-4.0, 16.0)[k]
    for j in range(10, 16):
        gown[j : j + 1, :] = jnp.zeros((1, FW), jnp.float32)
    ghost_copy = send(GHOST, gown, gnext, p, behind)
    top, bottom = OFF + (FA - 1) * PLANE, OFF

    def planes(n, relaxed):
        upward = send(
            n,
            relaxed.at[0:5, top : top + FR, :],
            relaxed.at[0:5, bottom - PLANE : bottom - PLANE + FR, :],
            p + 1,
            s,
        )
        downward = send(
            n + 1,
            relaxed.at[5:10, bottom : bottom + FR, :],
            relaxed.at[5:10, top + PLANE : top + PLANE + FR, :],
            p - 1,
            s,
        )
        return upward, downward

    def sides(n, box, there, chunks):
        groups = []
        for c, (row, size) in enumerate(chunks):
            at, to = pl.ds(row, size), pl.ds(8 + row, size)
            groups.append(
                [
                    send(n + 2 * c, box.at[1, :, at, :], there.at[0, :, to, :], p, ahead),
                    send(n + 2 * c + 1, box.at[0, :, at, :], there.at[1, :, to, :], p, behind),
                ]
            )
        return groups

    def start(group):
        for copy in group:
            copy.start()

    def arrive(group):
        for copy in group:
            copy.wait_recv()

    def leave(group):
        for copy in group:
            copy.wait_send()

    def axially(act, upward, downward, receiving):
        for there, group in (
            (has_low if receiving else has_high, upward),
            (has_high if receiving else has_low, downward),
        ):

            @pl.when(there)
            def _():
                act(group)

    sides1 = sides(FIRST, outbox, inbox, FIRST_ROWS)
    n = FIRST + 2 * CHUNKS
    plane_up1, plane_down1 = planes(n, relaxed1)
    small_up, small_down = [], []
    for group, m, coarse, row, there, edge in (
        (small_up, n + 2, p + 1, FA - 1, 7, 0),
        (small_down, n + 6, p - 1, 0, 40, 1),
    ):
        at = pl.ds(row, 1)
        to = pl.ds(there, 1)
        group += [
            send(m, outbox.at[1, 3:PARTS, at, :], inbox.at[0, 3:PARTS, to, :], coarse, ahead),
            send(m + 1, outbox.at[0, 3:PARTS, at, :], inbox.at[1, 3:PARTS, to, :], coarse, behind),
            send(m + 2, outbox.at[:, RIM_AT:PARTS, at, :], rims.at[:, :, to, :], coarse, s),
            send(m + 3, outbox.at[:, V_AT:RIM_AT, at, :], edges.at[edge], coarse, s),
        ]

    sides2 = sides(SECOND, sends, margin2, ALIGNED_ROWS)
    n = SECOND + 2 * CHUNKS
    plane_up2, plane_down2 = planes(n, relaxed2)
    corners_up, corners_down = [], []
    for group, m, coarse, row, there, j in (
        (corners_up, n + 2, p + 1, FA - 1, 7, 4),
        (corners_down, n + 4, p - 1, 0, 40, 3),
    ):
        at = pl.ds(row, 1)
        to = pl.ds(there, 1)
        group += [
            send(m, sends.at[1, j, at, :], margin2.at[0, j, to, :], coarse, ahead),
            send(m + 1, sends.at[0, j, at, :], margin2.at[1, j, to, :], coarse, behind),
        ]

    def keep_plane(relaxed, a, half, values, inside=False):
        rows = pl.ds(pl.multiple_of(OFF + a * PLANE + half * 8, 8), 8)
        for i in range(19):
            if inside:
                row = lax.broadcasted_iota(jnp.int32, (8, FW), 0)
                pltpu.store(relaxed.at[SLOT[i], rows, :], values[i], mask=row != 7 * half)
            else:
                relaxed[SLOT[i], rows, :] = values[i]

    def plane1(a, carry):
        for half in range(2):
            row = pl.multiple_of(a * FR + half * 8, 8)
            f = [fine[i, pl.ds(row, 8), :] for i in range(19)]
            push = [force[k, pl.ds(row, 8), :] for k in range(3)]
            keep_plane(relaxed1, a, half, collide(f, push, 1.0)[0])
        return carry

    def rim0(c):
        for side, r in ((0, 0), (1, FR - 1)):
            rows = pl.ds(c * (8 * FR) + r, 8, stride=FR)
            f = [fine[i, rows, :] for i in range(19)]
            push = [force[k, rows, :] for k in range(3)]
            values, u, inverse = collide(f, push, 1.0)
            cells = slice(c * 8, c * 8 + 8)
            for j, i in enumerate(FORTH if side else BACK):
                outbox[side, j, cells, :] = values[i]
            for k in range(3):
                outbox[side, V_AT + k, cells, :] = 3.0 * u[k] + 0.5625 * inverse * push[k]
            outbox[side, INVERSE_AT, cells, :] = inverse

    for c in range(4):
        loads[5 + c].wait()
        rim0(c)
    plane1(0, 0)
    plane1(FA - 1, 0)

    peers = 2 + jnp.where(has_low, 3, 0) + jnp.where(has_high, 3, 0)
    pl.semaphore_wait(barrier, peers)
    ghost_copy.start()
    axially(start, small_up, small_down, False)
    for c in (0, 3, 1, 2):
        start(sides1[c])
    axially(start, [plane_up1], [plane_down1], False)
    lax.fori_loop(1, FA - 1, plane1, 0, unroll=2)

    loads[3].wait()
    ghost_copy.wait_recv()
    window = jnp.concatenate([gown[...], gnext[...]], axis=1)
    turned = gmap[...]
    cell = lax.broadcasted_iota(jnp.int32, (FR, 2 * FW), 1)
    window_parts = split(window)
    for n in range(4):
        chosen = jnp.concatenate(
            [
                jnp.where(
                    jnp.broadcast_to(turned[:, a : a + 1], (FR, 2 * FW)) == cell, 1.0, 0.0
                )
                for a in range(n * 8, n * 8 + 8)
            ],
            axis=0,
        ).astype(jnp.bfloat16)
        total = jnp.zeros((128, 16), jnp.float32)
        for part in window_parts:
            total = total + lax.dot_general(
                chosen, part, (((1,), (1,)), ((), ())), preferred_element_type=jnp.float32
            )
        ghosts[n * 128 : n * 128 + 128, 0:16] = total

    def plane2(a, low, high):
        for half in range(2):
            f = pull_plane(relaxed1, ghosts, 0, a, half, low, high)
            row = pl.multiple_of(a * FR + half * 8, 8)
            push = [force[k, pl.ds(row, 8), :] for k in range(3)]
            keep_plane(relaxed2, a, half, collide(f, push, -0.25)[0], True)

    def inner2(a, carry):
        plane2(a, None, None)
        return carry

    def keep_rim(relaxed, a, r, values):
        row = OFF + a * PLANE + r
        for i in range(19):
            relaxed[SLOT[i], pl.ds(row, 8, stride=PLANE), :] = values[i]

    def whole_force(side, a, rows):
        cells = slice(8 + a, 16 + a)
        return [force[k, rows, :] + inbox[side, RIM_AT + k, cells, :] for k in range(3)]

    def rim1(a):
        for side, r in ((0, 0), (1, FR - 1)):
            rows = pl.ds(a * FR + r, 8, stride=FR)
            f = [fine[i, rows, :] for i in range(19)]
            keep_rim(relaxed1, a, r, collide(f, whole_force(side, a, rows), 1.0)[0])

    def rim2(c):
        for side, r in ((0, 0), (1, FR - 1)):
            f = pull_rim(relaxed1, margin1, ghosts, 0, c, r, first, last)
            rows = pl.ds(c * (8 * FR) + r, 8, stride=FR)
            values = collide(f, whole_force(side, c * 8, rows), -0.25)[0]
            keep_rim(relaxed2, c * 8, r, values)
            for j, i in enumerate(FORTH if side else BACK):
                sends[side, j, c * 8 : c * 8 + 8, :] = values[i]

    def margin_rows(side, cells, which):
        pops = [(BACK if side else FORTH)[j] for j in which]
        values = corrected(
            [inbox[side, j, cells, :] for j in which],
            pops,
            [rims[side, k, cells, :] for k in range(3)],
            [inbox[side, V_AT + k, cells, :] for k in range(3)],
            inbox[side, INVERSE_AT, cells, :],
        )
        for j, value in zip(which, values):
            margin1[side, j, cells, :] = value

    def edge_rows(edge, pops, plane, at):
        for side, r in ((0, 0), (1, FR - 1)):
            row = OFF + plane * PLANE + r
            values = corrected(
                [relaxed1[SLOT[i], row : row + 1, :] for i in pops],
                pops,
                [inbox[side, RIM_AT + k, at : at + 1, :] for k in range(3)],
                [edges[edge, side, k, :, :] for k in range(3)],
                edges[edge, side, 3, :, :],
            )
            for i, value in zip(pops, values):
                relaxed1[SLOT[i], row : row + 1, :] = value

    axially(arrive, [plane_up1], [plane_down1], True)
    axially(leave, [plane_up1], [plane_down1], False)
    def take(c):
        arrive(sides1[c])
        for a in FIRST_STARTS[c]:
            rim1(a)
            for side in range(2):
                margin_rows(side, slice(8 + a, 16 + a), range(5))

    take(0)
    take(3)
    axially(arrive, small_up, small_down, True)
    for side in range(2):
        margin_rows(side, slice(7, 8), [4])
        margin_rows(side, slice(40, 41), [3])
    edge_rows(0, UP, -1, 7)
    edge_rows(1, DOWN, FA, 40)
    rim2(0)
    axially(start, [], corners_down, False)
    start(sides2[0])
    rim2(3)
    axially(start, corners_up, [], False)
    start(sides2[3])
    for c in (1, 2):
        take(c)
        rim2(c)
        start(sides2[c])
    plane2(0, end_mask(first), None)
    plane2(FA - 1, None, end_mask(last))
    axially(start, [plane_up2], [plane_down2], False)
    lax.fori_loop(1, FA - 1, inner2, 0, unroll=5)
    ghost_copy.wait_send()
    for group in sides1:
        leave(group)
    axially(leave, small_up, small_down, False)
    axially(arrive, [plane_up2] + corners_up, [plane_down2] + corners_down, True)
    for group in sides2:
        arrive(group)
    for group in sides2:
        leave(group)
    axially(leave, [plane_up2] + corners_up, [plane_down2] + corners_down, False)


def settle(n_coarse, relaxed, margin, ghosts, out_hbm, out, sem):
    p = lax.axis_index("coarse")
    first, last = p == 0, p == n_coarse - 1

    def plane(a, low, high):
        for half in range(2):
            f = pull_plane(relaxed, ghosts, 5, a, half, low, high)
            row = pl.multiple_of(a * FR + half * 8, 8)
            for i in range(19):
                out[i, pl.ds(row, 8), :] = f[i] * 0.0625

    def inner(a, carry):
        plane(a, None, None)
        return carry

    copies = []
    for c in range(4):
        if c == 0:
            plane(0, end_mask(first), None)
        lax.fori_loop(max(c * 8, 1), min(c * 8 + 8, FA - 1), inner, 0, unroll=True)
        if c == 3:
            plane(FA - 1, None, end_mask(last))
        for r in (0, FR - 1):
            f = pull_rim(relaxed, margin, ghosts, 5, c, r, first, last)
            for i in range(19):
                out[i, pl.ds(c * (8 * FR) + r, 8, stride=FR), :] = f[i] * 0.0625
        rows = pl.ds(c * 128, 128)
        copy = pltpu.make_async_copy(out.at[:, rows, :], out_hbm.at[:, rows, :], sem.at[c])
        copy.start()
        copies.append(copy)
    for copy in copies:
        copy.wait()


def local(
    fine_populations,
    coarse_face,
    ghost_map,
    marker_force,
    marker_weights,
    marker_tiles,
    block_counts,
):
    n_coarse, n_sector = lax.axis_size("coarse"), lax.axis_size("sector")
    f32 = jnp.float32
    vmem = pl.BlockSpec(memory_space=pltpu.VMEM)
    hbm = pl.BlockSpec(memory_space=pltpu.HBM)
    margin = (2, 5, 48, FW)
    state = pl.pallas_call(
        functools.partial(advance, n_coarse, n_sector),
        out_shape=(
            pltpu.VMEM((19, ROWS, FW), f32),
            pltpu.VMEM(margin, f32),
            pltpu.VMEM((FA * FR, FW), f32),
        ),
        in_specs=[hbm] * 6 + [pl.BlockSpec(memory_space=pltpu.SMEM)],
        out_specs=(vmem, vmem, vmem),
        scratch_shapes=[
            pltpu.VMEM((19, FA * FR, FW), f32),
            pltpu.VMEM((19, 2, FW), f32),
            pltpu.VMEM((FR, FA), jnp.int32),
            pltpu.VMEM((3, NB, MB), jnp.bfloat16),
            pltpu.VMEM((NB, MB, FW), jnp.bfloat16),
            pltpu.SMEM((NB,), jnp.int32),
            pltpu.VMEM((NB * 8, MB), f32),
            pltpu.VMEM((NB * 8, FW), f32),
            pltpu.VMEM((3, FA * FR, FW), f32),
            pltpu.VMEM((2, 3, 48, FW), f32),
            pltpu.VMEM((16, FW), f32),
            pltpu.VMEM((16, FW), f32),
            pltpu.VMEM((19, ROWS, FW), f32),
            pltpu.VMEM(margin, f32),
            pltpu.VMEM((2, PARTS, FA, FW), f32),
            pltpu.VMEM((2, PARTS, 48, FW), f32),
            pltpu.VMEM((2, 2, 4, 1, FW), f32),
            pltpu.VMEM((2, 5, FA, FW), f32),
            pltpu.SemaphoreType.DMA((9,)),
            pltpu.SemaphoreType.DMA((N_REMOTE,)),
            pltpu.SemaphoreType.DMA((N_REMOTE,)),
        ],
        compiler_params=pltpu.CompilerParams(
            collective_id=0, has_side_effects=True, vmem_limit_bytes=32 * 1024 * 1024
        ),
        name="advance",
    )(
        *(
            pltpu.with_memory_space_constraint(x, pltpu.HBM)
            for x in (
                fine_populations.reshape(19, FA * FR, FW),
                jnp.transpose(coarse_face, (1, 0, 2)),
                jnp.transpose(ghost_map),
                jnp.transpose(marker_force, (1, 0, 2)),
                marker_weights,
                marker_tiles,
            )
        ),
        block_counts,
    )
    out = pl.pallas_call(
        functools.partial(settle, n_coarse),
        out_shape=jax.ShapeDtypeStruct((19, FA * FR, FW), f32),
        in_specs=[vmem, vmem, vmem],
        out_specs=hbm,
        scratch_shapes=[
            pltpu.VMEM((19, FA * FR, FW), f32),
            pltpu.SemaphoreType.DMA((4,)),
        ],
        compiler_params=pltpu.CompilerParams(vmem_limit_bytes=32 * 1024 * 1024),
        name="settle",
    )(*state)
    return out.reshape(19, FA, FR, FW)


def solution(mesh):
    in_specs = (
        P(None, "coarse", "sector", None),
        P(None, None, ("coarse", "sector")),
        P("coarse", "sector"),
        P(("coarse", "sector"), None, None),
        P(("coarse", "sector"), None, None),
        P(("coarse", "sector")),
        P(("coarse", "sector")),
    )
    out_specs = P(None, "coarse", "sector", None)
    return jax.shard_map(local, mesh=mesh, in_specs=in_specs, out_specs=out_specs, check_vma=False)
```

```python
import functools

import jax
import jax.numpy as jnp
from jax import lax
from jax.experimental import pallas as pl
from jax.experimental.pallas import tpu as pltpu
from jax.sharding import PartitionSpec as P

VELOCITIES = (
    (0, 0, 0),
    (1, 0, 0),
    (-1, 0, 0),
    (0, 1, 0),
    (0, -1, 0),
    (0, 0, 1),
    (0, 0, -1),
    (1, 1, 0),
    (-1, -1, 0),
    (1, -1, 0),
    (-1, 1, 0),
    (1, 0, 1),
    (-1, 0, -1),
    (1, 0, -1),
    (-1, 0, 1),
    (0, 1, 1),
    (0, -1, -1),
    (0, 1, -1),
    (0, -1, 1),
)
LATTICE_WEIGHTS = (1.0 / 3.0,) + (1.0 / 18.0,) * 6 + (1.0 / 36.0,) * 12
TAU_FINE = 0.8
TAU_COARSE = 0.65
FORCE_FACTOR = 1.0 - 0.5 / TAU_FINE
RESCALE = TAU_FINE / (2.0 * TAU_COARSE)

FA, FR, FW = 32, 16, 128
NB, MB = 32, 128
PLANE = 24
OFF = 32
ROWS = OFF + FA * PLANE + PLANE

UP = [i for i in range(19) if VELOCITIES[i][0] == 1]
DOWN = [i for i in range(19) if VELOCITIES[i][0] == -1]
FORTH = [3, 15, 17, 10, 7]
BACK = [4, 16, 18, 8, 9]
INWARD = [i for i in range(19) if VELOCITIES[i][2] == -1]
ORDER = UP + DOWN + [i for i in range(19) if VELOCITIES[i][0] == 0]
SLOT = {pop: slot for slot, pop in enumerate(ORDER)}

V_AT, INVERSE_AT, RIM_AT, PARTS = 5, 8, 9, 12

GHOST, FIRST, SECOND = 0, 1, 19
N_REMOTE = SECOND + 14
CHUNKS = 4
FIRST_ROWS = ((0, 9), (9, 8), (17, 6), (23, 9))
FIRST_STARTS = ((0, 1), (9,), (16,), (23, 24))
ALIGNED_ROWS = ((0, 8), (8, 8), (16, 8), (24, 8))

MESH = pl.DeviceIdType.MESH


def opposite(pop_index):
    if pop_index == 0:
        return 0
    return pop_index + 1 if pop_index % 2 == 1 else pop_index - 1


def collide(f, force, scale):
    gain = -4.0 / scale
    s, d = {}, {}
    for i in range(1, 19, 2):
        s[i] = f[i] + f[i + 1]
        d[i] = f[i] - f[i + 1]
    density = ((f[0] + s[1]) + (s[3] + s[5])) + ((s[7] + s[9]) + (s[11] + s[13])) + (s[15] + s[17])
    momentum = [
        d[1] + (d[7] + d[9]) + (d[11] + d[13]),
        d[3] + (d[7] - d[9]) + (d[15] + d[17]),
        d[5] + (d[11] - d[13]) + (d[15] - d[17]),
    ]
    guess = pl.reciprocal(density, approx=True)
    inverse = guess * (2.0 - density * guess)
    pushed = [momentum[k] + (0.5 / scale) * force[k] for k in range(3)]
    u = [pushed[k] * inverse for k in range(3)]
    h = [(-22.5 / 36.0) * pushed[k] + (gain * 3.375 / 36.0) * force[k] for k in range(3)]
    q = [(-15.0 / 36.0) * pushed[k] + (gain * 1.125 / 36.0) * force[k] for k in range(3)]
    t = [u[k] * h[k] for k in range(3)]
    base = (-5.0 / 36.0) * density - (1.0 / 3.0) * (t[0] + t[1] + t[2])
    out = [None] * 19
    out[0] = f[0] + 12.0 * base
    for k, i in enumerate((1, 3, 5)):
        even = 2.0 * (base + t[k])
        odd = 2.0 * q[k]
        out[i] = f[i] + (even + odd)
        out[i + 1] = f[i + 1] + (even - odd)
    for a, b, i in ((0, 1, 7), (0, 2, 11), (1, 2, 15)):
        common = base + t[a] + t[b]
        cross = u[a] * h[b] + u[b] * h[a]
        for j, even, odd in (
            (i, common + cross, q[a] + q[b]),
            (i + 2, common - cross, q[a] - q[b]),
        ):
            out[j] = f[j] + (even + odd)
            out[j + 1] = f[j + 1] + (even - odd)
    return out, u, inverse


def along(vector, i):
    terms = [vector[k] if VELOCITIES[i][k] == 1 else -vector[k] for k in range(3) if VELOCITIES[i][k]]
    return functools.reduce(lambda x, y: x + y, terms)


def corrected(base, pops, extra, v, inverse):
    w = [v[k] + 1.03125 * inverse * extra[k] for k in range(3)]
    shared = w[0] * extra[0] + w[1] * extra[1] + w[2] * extra[2]
    values = []
    for value, i in zip(base, pops):
        pushed = along(extra, i)
        grown = 3.0 * (pushed + along(w, i) * pushed) - shared
        values.append(value - (4.0 * LATTICE_WEIGHTS[i]) * grown)
    return values


def interface_rows(pops):
    density = pops[0]
    for i in range(1, 19):
        density = density + pops[i]
    velocity = []
    for k in range(3):
        running = jnp.zeros_like(density)
        for i in range(19):
            if VELOCITIES[i][k] == 1:
                running = running + pops[i]
            elif VELOCITIES[i][k] == -1:
                running = running - pops[i]
        velocity.append(running / density)
    speed_sq = velocity[0] * velocity[0] + velocity[1] * velocity[1] + velocity[2] * velocity[2]
    rows = []
    for i in INWARD:
        dotted = jnp.zeros_like(density)
        for k in range(3):
            if VELOCITIES[i][k] == 1:
                dotted = dotted + velocity[k]
            elif VELOCITIES[i][k] == -1:
                dotted = dotted - velocity[k]
        weight = LATTICE_WEIGHTS[i]
        balance = weight * density * (1.0 + 3.0 * dotted + 4.5 * dotted * dotted - 1.5 * speed_sq)
        rows.append(balance + RESCALE * (pops[i] - balance))
    return rows


def pulled(load, ghost, first_column, low, high):
    lane = lax.broadcasted_iota(jnp.int32, (8, FW), 1)
    inner = lane == 0
    outer = lane == FW - 1
    values = []
    for i in range(19):
        ca, cr, cw = VELOCITIES[i]
        value = load(i, -ca, -cr)
        ended = low if ca == 1 else high if ca == -1 else None
        if cw == 1 or ended is not None:
            reflected = load(opposite(i), 0, 0)
        if cw == 1:
            value = jnp.where(inner, reflected, pltpu.roll(value, 1, 1))
        elif cw == -1:
            shift = FW - 1 - (first_column + INWARD.index(i))
            value = jnp.where(outer, pltpu.roll(ghost, shift, 1), pltpu.roll(value, FW - 1, 1))
        if ended is not None:
            value = jnp.where(ended, reflected, value)
        values.append(value)
    return values


def pull_plane(relaxed, ghosts, first_column, a, half, low, high):
    row = OFF + a * PLANE + half * 8

    def load(i, da, dr):
        return relaxed[SLOT[i], pl.ds(row + da * PLANE + dr, 8), :]

    ghost = ghosts[pl.ds(a * FR + half * 8, 8), :]
    return pulled(load, ghost, first_column, low, high)


def pull_rim(relaxed, margin, ghosts, first_column, c, r, first, last):
    row = OFF + c * (8 * PLANE) + r

    def load(i, da, dr):
        if r + dr < 0:
            return margin[0, FORTH.index(i), pl.ds(8 + c * 8 + da, 8), :]
        if r + dr >= FR:
            return margin[1, BACK.index(i), pl.ds(8 + c * 8 + da, 8), :]
        return relaxed[SLOT[i], pl.ds(row + da * PLANE + dr, 8, stride=PLANE), :]

    ghost = ghosts[pl.ds(c * (8 * FR) + r, 8, stride=FR), :]
    axial = lax.broadcasted_iota(jnp.int32, (8, FW), 0) + c * 8
    low = axial == jnp.where(first, 0, -1)
    high = axial == jnp.where(last, FA - 1, -1)
    return pulled(load, ghost, first_column, low, high)


def end_mask(flag):
    return lax.broadcasted_iota(jnp.int32, (8, FW), 0) < jnp.where(flag, 8, 0)


def split(x):
    high = x.astype(jnp.bfloat16)
    rest = x - high.astype(jnp.float32)
    middle = rest.astype(jnp.bfloat16)
    low = (rest - middle.astype(jnp.float32)).astype(jnp.bfloat16)
    return high, middle, low


def advance(
    n_coarse,
    n_sector,
    fine_hbm,
    face_hbm,
    map_hbm,
    mforce_hbm,
    mweights_hbm,
    tiles_hbm,
    count_ref,
    relaxed2,
    margin2,
    ghosts,
    fine,
    face,
    gmap,
    mforce,
    mweights,
    tiles_ref,
    rows3,
    parts,
    force,
    rims,
    gown,
    gnext,
    relaxed1,
    margin1,
    outbox,
    inbox,
    edges,
    sends,
    local_sem,
    send_sem,
    recv_sem,
):
    p = lax.axis_index("coarse")
    s = lax.axis_index("sector")
    ahead = lax.rem(s + 1, n_sector)
    behind = lax.rem(s + n_sector - 1, n_sector)
    first, last = p == 0, p == n_coarse - 1
    has_low, has_high = p > 0, p < n_coarse - 1

    loads = [
        pltpu.make_async_copy(mweights_hbm, mweights, local_sem.at[0]),
        pltpu.make_async_copy(mforce_hbm, mforce, local_sem.at[1]),
        pltpu.make_async_copy(face_hbm, face, local_sem.at[2]),
        pltpu.make_async_copy(map_hbm, gmap, local_sem.at[3]),
        pltpu.make_async_copy(tiles_hbm, tiles_ref, local_sem.at[8]),
    ]
    for c in range(4):
        rows = pl.ds(c * 128, 128)
        loads.append(
            pltpu.make_async_copy(fine_hbm.at[:, rows, :], fine.at[:, rows, :], local_sem.at[4 + c])
        )
    for copy in loads:
        copy.start()

    barrier = pltpu.get_barrier_semaphore()

    def greet(coarse, sector):
        pl.semaphore_signal(
            barrier, inc=1, device_id={"coarse": coarse, "sector": sector}, device_id_type=MESH
        )

    greet(p, ahead)
    greet(p, behind)
    for there, coarse in ((has_low, p - 1), (has_high, p + 1)):

        @pl.when(there)
        def _():
            greet(coarse, s)
            greet(coarse, ahead)
            greet(coarse, behind)

    loads[1].wait()
    for k in range(3):
        rows3[pl.ds(k, NB, stride=8), :] = mforce[k].astype(jnp.float32)
    loads[0].wait()

    def block(b, carry):
        for k in range(4):
            n = b * 4 + k
            rows = pl.ds(pl.multiple_of(n * 8, 8), 8)
            parts[rows, :] = jnp.dot(
                rows3[rows, :].astype(jnp.bfloat16),
                mweights[n],
                preferred_element_type=jnp.float32,
            )
        return carry

    lax.fori_loop(0, NB // 4, block, 0)
    loads[4].wait()
    block_id = lax.rem(lax.broadcasted_iota(jnp.int32, (8, 3 * NB), 1), NB)
    tile = jnp.zeros((8, 3 * NB), jnp.int32)
    for b in range(NB):
        tile = jnp.where(block_id == b, tiles_ref[b], tile)
    axial = lax.shift_right_logical(tile * 3641, 16)
    cycle = tile - axial * (FR + 2)
    target = jnp.where(
        cycle == 0,
        FA * FR + axial,
        jnp.where(cycle == FR + 1, FA * FR + FA + axial, axial * FR + cycle - 1),
    )
    target = jnp.where(block_id < count_ref[0], target, -1)[:1]
    columns = []
    for k in range(3):
        high, middle, low = split(parts[pl.ds(k, NB, stride=8), :])
        columns.append(jnp.concatenate([high, middle, low], axis=0))
    columns = jnp.concatenate(columns, axis=1)
    for n in range(9):
        cell = lax.broadcasted_iota(jnp.int32, (64, 3 * NB), 0) + n * 64
        chosen = jnp.where(cell == target, 1.0, 0.0).astype(jnp.bfloat16)
        summed = jnp.dot(chosen, columns, preferred_element_type=jnp.float32)
        for k in range(3):
            column = summed[:, k * FW : k * FW + FW]
            if n < 8:
                force[k, n * 64 : n * 64 + 64, :] = column
            else:
                for side in range(2):
                    rim = column[side * FA : side * FA + FA]
                    rims[side, k, 8:40, :] = rim
                    outbox[side, RIM_AT + k, :, :] = rim

    def send(n, src, dst, coarse, sector):
        return pltpu.make_async_remote_copy(
            src_ref=src,
            dst_ref=dst,
            send_sem=send_sem.at[n],
            recv_sem=recv_sem.at[n],
            device_id={"coarse": coarse, "sector": sector},
            device_id_type=MESH,
        )

    loads[2].wait()
    for k in range(2):
        new = 0.5 * (k + 1)
        pops = [
            (1.0 - new) * face[i, 0:1, :] + new * face[i, 1:2, :] for i in range(19)
        ]
        for j, row in enumerate(interface_rows(pops)):
            gown[5 * k + j : 5 * k + j + 1, :] = row * (-4.0, 16.0)[k]
    for j in range(10, 16):
        gown[j : j + 1, :] = jnp.zeros((1, FW), jnp.float32)
    ghost_copy = send(GHOST, gown, gnext, p, behind)
    top, bottom = OFF + (FA - 1) * PLANE, OFF

    def planes(n, relaxed):
        upward = send(
            n,
            relaxed.at[0:5, top : top + FR, :],
            relaxed.at[0:5, bottom - PLANE : bottom - PLANE + FR, :],
            p + 1,
            s,
        )
        downward = send(
            n + 1,
            relaxed.at[5:10, bottom : bottom + FR, :],
            relaxed.at[5:10, top + PLANE : top + PLANE + FR, :],
            p - 1,
            s,
        )
        return upward, downward

    def sides(n, box, there, chunks):
        groups = []
        for c, (row, size) in enumerate(chunks):
            at, to = pl.ds(row, size), pl.ds(8 + row, size)
            groups.append(
                [
                    send(n + 2 * c, box.at[1, :, at, :], there.at[0, :, to, :], p, ahead),
                    send(n + 2 * c + 1, box.at[0, :, at, :], there.at[1, :, to, :], p, behind),
                ]
            )
        return groups

    def start(group):
        for copy in group:
            copy.start()

    def arrive(group):
        for copy in group:
            copy.wait_recv()

    def leave(group):
        for copy in group:
            copy.wait_send()

    def axially(act, upward, downward, receiving):
        for there, group in (
            (has_low if receiving else has_high, upward),
            (has_high if receiving else has_low, downward),
        ):

            @pl.when(there)
            def _():
                act(group)

    sides1 = sides(FIRST, outbox, inbox, FIRST_ROWS)
    n = FIRST + 2 * CHUNKS
    plane_up1, plane_down1 = planes(n, relaxed1)
    small_up, small_down = [], []
    for group, m, coarse, row, there, edge in (
        (small_up, n + 2, p + 1, FA - 1, 7, 0),
        (small_down, n + 6, p - 1, 0, 40, 1),
    ):
        at = pl.ds(row, 1)
        to = pl.ds(there, 1)
        group += [
            send(m, outbox.at[1, 3:PARTS, at, :], inbox.at[0, 3:PARTS, to, :], coarse, ahead),
            send(m + 1, outbox.at[0, 3:PARTS, at, :], inbox.at[1, 3:PARTS, to, :], coarse, behind),
            send(m + 2, outbox.at[:, RIM_AT:PARTS, at, :], rims.at[:, :, to, :], coarse, s),
            send(m + 3, outbox.at[:, V_AT:RIM_AT, at, :], edges.at[edge], coarse, s),
        ]

    sides2 = sides(SECOND, sends, margin2, ALIGNED_ROWS)
    n = SECOND + 2 * CHUNKS
    plane_up2, plane_down2 = planes(n, relaxed2)
    corners_up, corners_down = [], []
    for group, m, coarse, row, there, j in (
        (corners_up, n + 2, p + 1, FA - 1, 7, 4),
        (corners_down, n + 4, p - 1, 0, 40, 3),
    ):
        at = pl.ds(row, 1)
        to = pl.ds(there, 1)
        group += [
            send(m, sends.at[1, j, at, :], margin2.at[0, j, to, :], coarse, ahead),
            send(m + 1, sends.at[0, j, at, :], margin2.at[1, j, to, :], coarse, behind),
        ]

    def keep_plane(relaxed, a, half, values, inside=False):
        rows = pl.ds(pl.multiple_of(OFF + a * PLANE + half * 8, 8), 8)
        for i in range(19):
            if inside:
                row = lax.broadcasted_iota(jnp.int32, (8, FW), 0)
                pltpu.store(relaxed.at[SLOT[i], rows, :], values[i], mask=row != 7 * half)
            else:
                relaxed[SLOT[i], rows, :] = values[i]

    def plane1(a, carry):
        for half in range(2):
            row = pl.multiple_of(a * FR + half * 8, 8)
            f = [fine[i, pl.ds(row, 8), :] for i in range(19)]
            push = [force[k, pl.ds(row, 8), :] for k in range(3)]
            keep_plane(relaxed1, a, half, collide(f, push, 1.0)[0])
        return carry

    def rim0(c):
        for side, r in ((0, 0), (1, FR - 1)):
            rows = pl.ds(c * (8 * FR) + r, 8, stride=FR)
            f = [fine[i, rows, :] for i in range(19)]
            push = [force[k, rows, :] for k in range(3)]
            values, u, inverse = collide(f, push, 1.0)
            cells = slice(c * 8, c * 8 + 8)
            for j, i in enumerate(FORTH if side else BACK):
                outbox[side, j, cells, :] = values[i]
            for k in range(3):
                outbox[side, V_AT + k, cells, :] = 3.0 * u[k] + 0.5625 * inverse * push[k]
            outbox[side, INVERSE_AT, cells, :] = inverse

    for c in range(4):
        loads[5 + c].wait()
        rim0(c)
    plane1(0, 0)
    plane1(FA - 1, 0)

    peers = 2 + jnp.where(has_low, 3, 0) + jnp.where(has_high, 3, 0)
    pl.semaphore_wait(barrier, peers)
    ghost_copy.start()
    start(sides1[0])
    axially(start, small_up, small_down, False)
    for c in (3, 1, 2):
        start(sides1[c])
    axially(start, [plane_up1], [plane_down1], False)
    lax.fori_loop(1, FA - 1, plane1, 0, unroll=2)

    loads[3].wait()
    ghost_copy.wait_recv()
    window = jnp.concatenate([gown[...], gnext[...]], axis=1)
    turned = gmap[...]
    cell = lax.broadcasted_iota(jnp.int32, (FR, 2 * FW), 1)
    window_parts = split(window)
    for n in range(4):
        chosen = jnp.concatenate(
            [
                jnp.where(
                    jnp.broadcast_to(turned[:, a : a + 1], (FR, 2 * FW)) == cell, 1.0, 0.0
                )
                for a in range(n * 8, n * 8 + 8)
            ],
            axis=0,
        ).astype(jnp.bfloat16)
        total = jnp.zeros((128, 16), jnp.float32)
        for part in window_parts:
            total = total + lax.dot_general(
                chosen, part, (((1,), (1,)), ((), ())), preferred_element_type=jnp.float32
            )
        ghosts[n * 128 : n * 128 + 128, 0:16] = total

    def plane2(a, low, high):
        for half in range(2):
            f = pull_plane(relaxed1, ghosts, 0, a, half, low, high)
            row = pl.multiple_of(a * FR + half * 8, 8)
            push = [force[k, pl.ds(row, 8), :] for k in range(3)]
            keep_plane(relaxed2, a, half, collide(f, push, -0.25)[0], True)

    def inner2(a, carry):
        plane2(a, None, None)
        return carry

    def keep_rim(relaxed, a, r, values):
        row = OFF + a * PLANE + r
        for i in range(19):
            relaxed[SLOT[i], pl.ds(row, 8, stride=PLANE), :] = values[i]

    def whole_force(side, a, rows):
        cells = slice(8 + a, 16 + a)
        return [force[k, rows, :] + inbox[side, RIM_AT + k, cells, :] for k in range(3)]

    def rim1(a):
        for side, r in ((0, 0), (1, FR - 1)):
            rows = pl.ds(a * FR + r, 8, stride=FR)
            f = [fine[i, rows, :] for i in range(19)]
            keep_rim(relaxed1, a, r, collide(f, whole_force(side, a, rows), 1.0)[0])

    def rim2(c):
        for side, r in ((0, 0), (1, FR - 1)):
            f = pull_rim(relaxed1, margin1, ghosts, 0, c, r, first, last)
            rows = pl.ds(c * (8 * FR) + r, 8, stride=FR)
            values = collide(f, whole_force(side, c * 8, rows), -0.25)[0]
            keep_rim(relaxed2, c * 8, r, values)
            for j, i in enumerate(FORTH if side else BACK):
                sends[side, j, c * 8 : c * 8 + 8, :] = values[i]

    def margin_rows(side, cells, which):
        pops = [(BACK if side else FORTH)[j] for j in which]
        values = corrected(
            [inbox[side, j, cells, :] for j in which],
            pops,
            [rims[side, k, cells, :] for k in range(3)],
            [inbox[side, V_AT + k, cells, :] for k in range(3)],
            inbox[side, INVERSE_AT, cells, :],
        )
        for j, value in zip(which, values):
            margin1[side, j, cells, :] = value

    def edge_rows(edge, pops, plane, at):
        for side, r in ((0, 0), (1, FR - 1)):
            row = OFF + plane * PLANE + r
            values = corrected(
                [relaxed1[SLOT[i], row : row + 1, :] for i in pops],
                pops,
                [inbox[side, RIM_AT + k, at : at + 1, :] for k in range(3)],
                [edges[edge, side, k, :, :] for k in range(3)],
                edges[edge, side, 3, :, :],
            )
            for i, value in zip(pops, values):
                relaxed1[SLOT[i], row : row + 1, :] = value

    axially(arrive, [plane_up1], [plane_down1], True)
    axially(leave, [plane_up1], [plane_down1], False)
    def take(c):
        arrive(sides1[c])
        for a in FIRST_STARTS[c]:
            rim1(a)
            for side in range(2):
                margin_rows(side, slice(8 + a, 16 + a), range(5))

    take(0)
    axially(arrive, small_up, small_down, True)
    for side in range(2):
        margin_rows(side, slice(7, 8), [4])
        margin_rows(side, slice(40, 41), [3])
    edge_rows(0, UP, -1, 7)
    edge_rows(1, DOWN, FA, 40)
    take(3)
    rim2(0)
    axially(start, [], corners_down, False)
    start(sides2[0])
    rim2(3)
    axially(start, corners_up, [], False)
    start(sides2[3])
    for c in (1, 2):
        take(c)
        rim2(c)
        start(sides2[c])
    plane2(0, end_mask(first), None)
    plane2(FA - 1, None, end_mask(last))
    axially(start, [plane_up2], [plane_down2], False)
    lax.fori_loop(1, FA - 1, inner2, 0, unroll=5)
    ghost_copy.wait_send()
    for group in sides1:
        leave(group)
    axially(leave, small_up, small_down, False)
    axially(arrive, [plane_up2] + corners_up, [plane_down2] + corners_down, True)
    for group in sides2:
        arrive(group)
    for group in sides2:
        leave(group)
    axially(leave, [plane_up2] + corners_up, [plane_down2] + corners_down, False)


def settle(n_coarse, relaxed, margin, ghosts, out_hbm, out, sem):
    p = lax.axis_index("coarse")
    first, last = p == 0, p == n_coarse - 1

    def plane(a, low, high):
        for half in range(2):
            f = pull_plane(relaxed, ghosts, 5, a, half, low, high)
            row = pl.multiple_of(a * FR + half * 8, 8)
            for i in range(19):
                out[i, pl.ds(row, 8), :] = f[i] * 0.0625

    def inner(a, carry):
        plane(a, None, None)
        return carry

    copies = []
    for c in range(4):
        if c == 0:
            plane(0, end_mask(first), None)
        lax.fori_loop(max(c * 8, 1), min(c * 8 + 8, FA - 1), inner, 0, unroll=True)
        if c == 3:
            plane(FA - 1, None, end_mask(last))
        for r in (0, FR - 1):
            f = pull_rim(relaxed, margin, ghosts, 5, c, r, first, last)
            for i in range(19):
                out[i, pl.ds(c * (8 * FR) + r, 8, stride=FR), :] = f[i] * 0.0625
        rows = pl.ds(c * 128, 128)
        copy = pltpu.make_async_copy(out.at[:, rows, :], out_hbm.at[:, rows, :], sem.at[c])
        copy.start()
        copies.append(copy)
    for copy in copies:
        copy.wait()


def local(
    fine_populations,
    coarse_face,
    ghost_map,
    marker_force,
    marker_weights,
    marker_tiles,
    block_counts,
):
    n_coarse, n_sector = lax.axis_size("coarse"), lax.axis_size("sector")
    f32 = jnp.float32
    vmem = pl.BlockSpec(memory_space=pltpu.VMEM)
    hbm = pl.BlockSpec(memory_space=pltpu.HBM)
    margin = (2, 5, 48, FW)
    state = pl.pallas_call(
        functools.partial(advance, n_coarse, n_sector),
        out_shape=(
            pltpu.VMEM((19, ROWS, FW), f32),
            pltpu.VMEM(margin, f32),
            pltpu.VMEM((FA * FR, FW), f32),
        ),
        in_specs=[hbm] * 6 + [pl.BlockSpec(memory_space=pltpu.SMEM)],
        out_specs=(vmem, vmem, vmem),
        scratch_shapes=[
            pltpu.VMEM((19, FA * FR, FW), f32),
            pltpu.VMEM((19, 2, FW), f32),
            pltpu.VMEM((FR, FA), jnp.int32),
            pltpu.VMEM((3, NB, MB), jnp.bfloat16),
            pltpu.VMEM((NB, MB, FW), jnp.bfloat16),
            pltpu.SMEM((NB,), jnp.int32),
            pltpu.VMEM((NB * 8, MB), f32),
            pltpu.VMEM((NB * 8, FW), f32),
            pltpu.VMEM((3, FA * FR, FW), f32),
            pltpu.VMEM((2, 3, 48, FW), f32),
            pltpu.VMEM((16, FW), f32),
            pltpu.VMEM((16, FW), f32),
            pltpu.VMEM((19, ROWS, FW), f32),
            pltpu.VMEM(margin, f32),
            pltpu.VMEM((2, PARTS, FA, FW), f32),
            pltpu.VMEM((2, PARTS, 48, FW), f32),
            pltpu.VMEM((2, 2, 4, 1, FW), f32),
            pltpu.VMEM((2, 5, FA, FW), f32),
            pltpu.SemaphoreType.DMA((9,)),
            pltpu.SemaphoreType.DMA((N_REMOTE,)),
            pltpu.SemaphoreType.DMA((N_REMOTE,)),
        ],
        compiler_params=pltpu.CompilerParams(
            collective_id=0, has_side_effects=True, vmem_limit_bytes=32 * 1024 * 1024
        ),
        name="advance",
    )(
        *(
            pltpu.with_memory_space_constraint(x, pltpu.HBM)
            for x in (
                fine_populations.reshape(19, FA * FR, FW),
                jnp.transpose(coarse_face, (1, 0, 2)),
                jnp.transpose(ghost_map),
                jnp.transpose(marker_force, (1, 0, 2)),
                marker_weights,
                marker_tiles,
            )
        ),
        block_counts,
    )
    out = pl.pallas_call(
        functools.partial(settle, n_coarse),
        out_shape=jax.ShapeDtypeStruct((19, FA * FR, FW), f32),
        in_specs=[vmem, vmem, vmem],
        out_specs=hbm,
        scratch_shapes=[
            pltpu.VMEM((19, FA * FR, FW), f32),
            pltpu.SemaphoreType.DMA((4,)),
        ],
        compiler_params=pltpu.CompilerParams(vmem_limit_bytes=32 * 1024 * 1024),
        name="settle",
    )(*state)
    return out.reshape(19, FA, FR, FW)


def solution(mesh):
    in_specs = (
        P(None, "coarse", "sector", None),
        P(None, None, ("coarse", "sector")),
        P("coarse", "sector"),
        P(("coarse", "sector"), None, None),
        P(("coarse", "sector"), None, None),
        P(("coarse", "sector")),
        P(("coarse", "sector")),
    )
    out_specs = P(None, "coarse", "sector", None)
    return jax.shard_map(local, mesh=mesh, in_specs=in_specs, out_specs=out_specs, check_vma=False)
```
